256 devices in a mesh: cohort: 4 (over y), gene: 64 (over x, z, core).
Axes of the slice: x: 4, y: 4, z: 8, core: 2. Of those that a mesh axis runs over, the one named last changes fastest.
Arguments:
- scores: bfloat16 [4, 393216, 512], P('cohort', 'gene'), may hold values from -6 to 6
- flips: int32 [4, 393216], P('cohort', 'gene'), may hold values from 0 to 1
- presence: int32 [4, 393216], P('cohort', 'gene'), may hold values 0 or 1
- covs: bfloat16 [4, 3072, 128, 128], P('cohort', 'gene'), may hold values from -2 to 2.5, as said below
- membership: int32 [8, 393216], P(None, 'gene'), may hold values 0 or 1
- weights: float32 [393216], P('gene'), may hold values from 0.25 to 4
- tile_owner: int32 [3072, 1], P('gene'), may hold values from 0 to 63; in each aligned block of 48 rows (0 to 47, 48 to 95, ...) at most 2 rows name the same one
- tile_gene: int32 [3072], P('gene'), may hold values from 0 to 15
Outputs:
- burden_z: float32 [1024, 8, 512], P('gene', None, 'cohort')
- skat_z: float32 [1024, 8, 512], P('gene', None, 'cohort')
The draws below stay inside these ranges and needn't reach their ends.
Inputs may be any that keep to these rules, and one draw needn't show every extreme that they name: `tile_owner`: in the tiles of one device (aligned blocks of 48 tiles) at most 2 belong to one owner. `covs`: each block is symmetric.
All inputs are finite; a program needn't handle non-finite values. No bound on the sum of `presence` or of `membership` on one device may be relied on, other than what follows from the above.
Results may differ from the reference program's by a relative error of at most 0.035.
Values may be sent and summed in bfloat16 or wider, within the bound.
A program may use at most 128 MiB of HBM per device.

```python
import math
import jax
import jax.numpy as jnp
import numpy as np
from jax import lax

VT = 128
P_SIZE = 512
MASKS = 8
TILE_DEV = 48
GENE_DEV = 16
COHORTS = 4
TILES = 3072
VARIANTS = 393216
GENES = 1024
CAP = 2
N_GENE = 64


def flip_bits(key):
    return jax.random.randint(jax.random.fold_in(key, 101), (COHORTS, VARIANTS), 0, 2, dtype=jnp.int32)


def draw_flips(key, part):
    return flip_bits(key)


def draw_covs(key, part):
    base = jax.random.fold_in(key, 202)
    scale_key, nugget_key, length_key, rough_key = jax.random.split(base, 4)
    allele_sign = (1.0 - 2.0 * flip_bits(key).astype(jnp.float32)).reshape(COHORTS, TILES, VT)
    position = jnp.arange(VT, dtype=jnp.float32)
    distance = jnp.abs(position[:, None] - position[None, :])
    length = VT * jax.random.uniform(length_key, (COHORTS, TILES, 1, 1), jnp.float32, 0.06, 0.4)
    rough = jax.random.uniform(rough_key, (COHORTS, TILES, VT, VT), jnp.float32, 0.0, 0.6)
    rough = 0.5 * (rough + jnp.swapaxes(rough, 2, 3))
    scale = jax.random.uniform(scale_key, (COHORTS, TILES, VT), jnp.float32, 0.75, 1.25)
    nugget = jax.random.uniform(nugget_key, (COHORTS, TILES, VT), jnp.float32, 0.1, 0.4)
    envelope = jnp.exp(-distance / length)
    identity = jnp.eye(VT, dtype=jnp.float32)
    shared = envelope * (1.0 - rough) * (1.0 - identity) + identity * (1.0 + nugget[:, :, :, None])
    signed_scale = scale * allele_sign
    blocks = signed_scale[:, :, :, None] * signed_scale[:, :, None, :] * shared
    return blocks.astype(jnp.bfloat16)


def with_ends(result, own_key, smallest, top_value):
    longest = result.shape.index(max(result.shape))
    spots = []
    for shift in (0, 1):
        where = [jax.random.randint(jax.random.fold_in(own_key, axis), (), 0, length) for axis, length in enumerate(result.shape)]
        where[longest] = (where[longest] + shift) % result.shape[longest]
        spots.append(tuple(where))
    return result.at[spots[0]].set(smallest).at[spots[1]].set(top_value)


def shard_levels(stream_key, extent, cuts, low, high):
    def one(dim, blocks):
        heights = jax.random.uniform(jax.random.fold_in(jax.random.fold_in(stream_key, 6), dim), (blocks,), jnp.float32, low / len(cuts), high / len(cuts))
        return jnp.repeat(jnp.exp(heights), extent[dim] // blocks).reshape((-1,) + (1,) * (len(extent) - dim - 1))

    level = one(*cuts[0])
    for cut in cuts[1:]:
        level = level * one(*cut)
    return level


def shared_out(key, own, number, rows, number_of, top, most, skew):
    order = jax.random.permutation(key, number_of)
    crowded, ordinary = load_shares(number_of, rows * top, most, skew, True), load_shares(number_of, rows * top, most, skew, False)
    places = jnp.arange(number_of)

    def named(tallies, rotation):
        used = int((tallies > 0).sum())
        fixed = max(1, used // 4)
        shifted = fixed + (places - fixed + rotation * (used - fixed)) % max(1, number_of - fixed)
        return jnp.zeros((number_of,), jnp.int32).at[order[jnp.where(places < fixed, places, shifted)]].set(jnp.asarray(tallies, jnp.int32))

    tallies = jnp.where(number % 4 == 0, named(crowded, number // 4), named(ordinary, number - number // 4 - 1))
    mixed = jax.random.permutation(jax.random.fold_in(own, 3), number_of)
    donor, taker = mixed[0:number_of // 2 * 2:2], mixed[1:number_of // 2 * 2:2]
    slack = jnp.minimum(tallies[donor] - 1, most - tallies[taker]) // 2
    slack = jnp.where((donor == order[0]) | (taker == order[0]) | (tallies[taker] == 0), 0, jnp.maximum(slack, 0))
    shifted = jax.random.randint(jax.random.fold_in(own, 4), (number_of // 2,), 0, 1 << 20) % (slack + 1)
    tallies = tallies.at[donor].add(-shifted).at[taker].add(shifted)
    items = jnp.searchsorted(jnp.cumsum(tallies), jnp.arange(rows * top), side="right").astype(jnp.int32)
    grid = items.reshape(top, rows).T
    grid = grid[jax.random.permutation(jax.random.fold_in(own, 1), rows)]
    rotation = jax.random.randint(jax.random.fold_in(own, 2), (rows, 1), 0, top)
    return jnp.take_along_axis(grid, (jnp.arange(top)[None, :] + rotation) % top, axis=1)


def load_shares(amount, total, most, skew, full):
    loads = [(1 << 20) // math.isqrt(rank ** skew) + 1 for rank in range(1, amount + 1)]
    largest = most if full else min(most, max(-(-total // amount), total * loads[0] // sum(loads)))
    least = 1 if total - largest >= amount - 1 else 0
    holding, rest = [largest] + [least] * (amount - 1), total - largest - least * (amount - 1)
    while rest > 0:
        free = [i for i in range(1, amount) if holding[i] < largest] or [i for i in range(1, amount) if holding[i] < most]
        mass, budget = sum([loads[i] for i in free]), rest
        for i in free:
            more = min(most - holding[i], max(1, budget * loads[i] // mass), rest)
            holding[i] = holding[i] + more
            rest = rest - more
    return np.array(holding)


def centred(own_key, shape, scale, bound, shards=(), kind=jnp.bfloat16):
    values = scale * jax.random.normal(own_key, shape, jnp.float32)
    if shards:
        values = values * shard_levels(own_key, shape, shards, -0.22, 0.18)
    return jnp.clip(values, -bound, bound).astype(kind)


def setup_inputs(seed: int = 0) -> dict:
    splits = jax.random.split(jax.random.key(seed), 9)
    scores = centred(splits[0], (COHORTS, VARIANTS, P_SIZE), 1.2, 6.0, ((0, 4), (1, 64)))
    flips = draw_flips(jax.random.fold_in(splits[8], 71), 0)
    presence = with_ends((jax.random.randint(splits[2], (COHORTS, VARIANTS), 0, 8) < 7).astype(jnp.int32), jax.random.fold_in(splits[2], 1), 0, 1)
    covs = draw_covs(jax.random.fold_in(splits[8], 71), 0)
    membership = with_ends((jax.random.randint(splits[4], (MASKS, VARIANTS), 0, 2) < 1).astype(jnp.int32), jax.random.fold_in(splits[4], 1), 0, 1)
    weights = jnp.clip(jnp.exp(math.log(4.0) - 2.7725887 * jax.random.uniform(splits[5], (VARIANTS,), jnp.float32) ** shard_levels(splits[5], (VARIANTS,), ((0, 64),), -0.2, 0.2)), 0.25, 4.0)
    tile_owner_keys = jax.random.split(jax.random.fold_in(splits[6], 1), TILES // TILE_DEV)
    tile_owner_turns = jax.random.permutation(jax.random.fold_in(splits[6], 3), TILES // TILE_DEV)
    tile_owner = jax.vmap(lambda own, number: shared_out(jax.random.fold_in(splits[6], 2), own, number, TILE_DEV, N_GENE, 1, CAP, 2))(tile_owner_keys, tile_owner_turns).reshape((TILES, 1))
    tile_gene = with_ends(jax.random.randint(splits[7], (TILES,), 0, GENE_DEV), jax.random.fold_in(splits[7], 1), 0, GENE_DEV - 1).astype(jnp.int32)
    return {"scores": scores, "flips": flips, "presence": presence, "covs": covs, "membership": membership, "weights": weights, "tile_owner": tile_owner, "tile_gene": tile_gene}


def group_stats(position, scores, flips, presence, covs, membership, weights):
    variant_span = TILE_DEV * VT
    first_row = (position * variant_span).astype(jnp.int32)
    first_tile = (position * TILE_DEV).astype(jnp.int32)
    score_part = lax.dynamic_slice_in_dim(scores, first_row, variant_span, 1).astype(jnp.float32)
    flip_part = lax.dynamic_slice_in_dim(flips, first_row, variant_span, 1).astype(jnp.float32)
    present_part = lax.dynamic_slice_in_dim(presence, first_row, variant_span, 1).astype(jnp.float32)
    cov_part = lax.dynamic_slice_in_dim(covs, first_tile, TILE_DEV, 1).astype(jnp.float32)
    member_part = lax.dynamic_slice_in_dim(membership, first_row, variant_span, 1).astype(jnp.float32)
    weight_part = lax.dynamic_slice_in_dim(weights, first_row, variant_span, 0)
    allele_sign = 1.0 - 2.0 * flip_part
    factor = allele_sign * present_part
    united = lax.optimization_barrier(jnp.sum(score_part * factor[:, :, None], axis=0)).astype(jnp.bfloat16)
    united = lax.optimization_barrier(united)
    tile_sign = allele_sign.reshape(COHORTS, TILE_DEV, VT)
    blocks = lax.optimization_barrier(jnp.sum(tile_sign[:, :, :, None] * tile_sign[:, :, None, :] * cov_part, axis=0)).astype(jnp.bfloat16)
    blocks = lax.optimization_barrier(blocks)
    mask_weights = (weight_part[None, :] * (1.0 + 3.0 * member_part) / 4.0).astype(jnp.bfloat16)
    mask_weights = lax.optimization_barrier(mask_weights)
    w_wide = jnp.transpose(mask_weights.reshape(MASKS, TILE_DEV, VT), (1, 0, 2)).astype(jnp.float32)
    u_wide = united.reshape(TILE_DEV, VT, P_SIZE).astype(jnp.float32)
    w_square = w_wide * w_wide
    tile_burden = jnp.einsum('kmv,kvp->kmp', w_wide, u_wide, precision=lax.Precision.HIGHEST)
    tile_square = jnp.einsum('kmv,kvp->kmp', w_square, u_wide * u_wide, precision=lax.Precision.HIGHEST)
    v_wide = blocks.astype(jnp.float32)
    carried = jnp.einsum('kij,kmj->kmi', v_wide, w_wide, precision=lax.Precision.HIGHEST)
    tile_variance = lax.optimization_barrier(jnp.sum(carried * w_wide, axis=2))
    diagonal = jnp.diagonal(v_wide, axis1=1, axis2=2)
    tile_trace = lax.optimization_barrier(jnp.sum(w_square * diagonal[:, None, :], axis=2))
    squared = jnp.einsum('kij,kmj->kmi', v_wide * v_wide, w_square, precision=lax.Precision.HIGHEST)
    tile_spread = lax.optimization_barrier(jnp.sum(squared * w_square, axis=2))
    return (tile_burden, tile_square, tile_variance, tile_trace, tile_spread)

def reference(scores, flips, presence, covs, membership, weights, tile_owner, tile_gene):

    def one_group(position):
        return group_stats(position, scores, flips, presence, covs, membership, weights)
    results = lax.map(one_group, jnp.arange(N_GENE, dtype=jnp.int32))
    tile_burden, tile_square, tile_variance, tile_trace, tile_spread = [value.reshape((TILES,) + value.shape[2:]) for value in results]
    gene_ids = (tile_owner[:, 0] * GENE_DEV + tile_gene).astype(jnp.int32)
    gene_burden = jax.ops.segment_sum(tile_burden, gene_ids, num_segments=GENES)
    gene_square = jax.ops.segment_sum(tile_square, gene_ids, num_segments=GENES)
    gene_variance = jax.ops.segment_sum(tile_variance, gene_ids, num_segments=GENES)
    gene_trace = jax.ops.segment_sum(tile_trace, gene_ids, num_segments=GENES)
    gene_spread = jax.ops.segment_sum(tile_spread, gene_ids, num_segments=GENES)
    burden_z = gene_burden / jnp.sqrt(jnp.maximum(gene_variance, 1.0))[:, :, None]
    skat_z = (gene_square - gene_trace[:, :, None]) / jnp.sqrt(jnp.maximum(2.0 * gene_spread, 1.0))[:, :, None]
    return (burden_z, skat_z)
```

```python
import functools

import jax
import jax.numpy as jnp
from jax import lax
from jax.experimental import pallas as pl
from jax.experimental.pallas import tpu as pltpu
from jax.sharding import PartitionSpec as P

F32, BF16 = jnp.float32, jnp.bfloat16
MESH = pl.DeviceIdType.MESH
TILE = 128
TILES = 48
HALF = TILES // 2
CHUNKS = 4
CHUNK_TILES = HALF // CHUNKS
CHUNK_ROWS = CHUNK_TILES * TILE
COHORTS = 4
OWNERS = 64
GENES = 16
MASKS = 8
OWN_TILES = TILES // COHORTS
PAIRS = OWN_TILES // 2
COV_ROWS = PAIRS // 2 * TILE + 16
HIGHEST = lax.Precision.HIGHEST


def rows_of(tile):
    return pl.ds(pl.multiple_of(tile * TILE, TILE), TILE)


def iota(axis, shape=(TILE, TILE)):
    return lax.broadcasted_iota(jnp.int32, shape, axis)


def kernel(
    scores, flips, presence, covs, membership, weights, owner, gene,
    burden_out, skat_out,
    buf, got, factor_wide, cov_in, cov_out, cov_got, factor, sign, held,
    var_mine, var_got, spread_mine, spread_got, stats, stats_got,
    wide, packed, arrived, wide_got,
    load_sem, cov_sem, send_sem, recv_sem, cov_send, cov_recv,
    var_send, var_recv, spread_send, spread_recv, stat_send, stat_recv, pay_send, pay_recv,
):
    me = lax.axis_index("cohort")
    mine = lax.axis_index("gene")

    def cohort(relative):
        return lax.rem(me + relative, COHORTS)

    def owner_at(offset):
        return lax.rem(mine + offset, OWNERS)

    def load(relative):
        columns = pl.ds(pl.multiple_of(cohort(relative) * TILE, TILE), TILE)
        return pltpu.make_async_copy(scores.at[0, :, columns], buf.at[relative], load_sem.at[relative])

    load_cov = pltpu.make_async_copy(covs.at[0], cov_in, cov_sem)
    load(2).start()
    load(1).start()
    load(3).start()
    load_cov.start()
    load(0).start()

    barrier = pltpu.get_barrier_semaphore()
    for step in range(1, COHORTS):
        pl.semaphore_signal(barrier, inc=1, device_id={"cohort": cohort(step)}, device_id_type=MESH)

    def greet(offset, carry):
        pl.semaphore_signal(barrier, inc=1, device_id={"gene": owner_at(offset)}, device_id_type=MESH)
        return carry

    lax.fori_loop(1, OWNERS, greet, 0)

    sign[...] = 1.0 - 2.0 * flips[...].astype(F32)
    factor[...] = sign[...] * presence[...].astype(F32)
    held[...] = jnp.zeros_like(held)

    owner_row = jnp.full((1, TILE), -1.0, F32)
    owner_row = jnp.concatenate([owner[...].astype(F32), owner_row[:, :TILE - TILES]], axis=1)
    gene_row = jnp.concatenate([gene[...].astype(F32) + 1.0, jnp.zeros((1, TILE - TILES), F32)], axis=1)
    owner_rows = jnp.broadcast_to(owner_row, (TILE, TILE))
    same = (owner_rows == owner_rows.T) & (iota(0) < iota(1))
    rank_row = jnp.sum(same.astype(F32), axis=0, keepdims=True)
    slot_row = jnp.where(owner_row >= 0.0, owner_row + OWNERS * rank_row, -1.0)
    slots = (slot_row == iota(0).astype(F32)).astype(F32)

    def piece(way, phase, chunk):
        half = 1 - way if phase == 1 else way
        relative = 2 if phase == 0 else (1 if way == 0 else 3)
        first = pl.multiple_of((half * HALF + chunk * CHUNK_TILES) * TILE, TILE)
        landing = pl.multiple_of(chunk * CHUNK_ROWS, TILE)
        return pltpu.make_async_remote_copy(
            src_ref=buf.at[relative, pl.ds(first, CHUNK_ROWS)],
            dst_ref=got.at[phase, way, pl.ds(landing, CHUNK_ROWS)],
            send_sem=send_sem.at[way, phase, chunk],
            recv_sem=recv_sem.at[way, phase, chunk],
            device_id={"cohort": cohort(1 if way == 0 else 3)},
            device_id_type=MESH,
        )

    def cov_piece(way, phase):
        half = 1 - way if phase == 1 else way
        relative = 2 if phase == 0 else (1 if way == 0 else 3)
        return pltpu.make_async_remote_copy(
            src_ref=cov_out.at[cohort(relative), half],
            dst_ref=cov_got.at[phase, way],
            send_sem=cov_send.at[way, phase],
            recv_sem=cov_recv.at[way, phase],
            device_id={"cohort": cohort(1 if way == 0 else 3)},
            device_id_type=MESH,
        )

    def mask_weights(tile):
        member = membership[:, rows_of(tile)].astype(F32)
        return (weights[pl.ds(tile, 1), :] * (1.0 + 3.0 * member) / 4.0).astype(BF16)

    load(2).wait()
    pl.semaphore_wait(barrier, OWNERS - 1 + COHORTS - 1)

    def far(chunk, carry):
        for way in range(2):
            def one(k, inner):
                tile = way * HALF + chunk * CHUNK_TILES + k
                rows = rows_of(tile)
                column = jnp.broadcast_to(factor[pl.ds(tile, 1), :], (TILE, TILE)).T
                factor_wide[rows, :] = column.astype(BF16)
                buf[2, rows, :] = (buf[2, rows, :].astype(F32) * column).astype(BF16)
                return inner

            lax.fori_loop(0, CHUNK_TILES, one, 0)
            piece(way, 0, chunk).start()
        return carry

    lax.fori_loop(0, CHUNKS, far, 0)

    load_cov.wait()
    lane = iota(1, (MASKS, TILE))

    def cov_group(group, linear):
        root, half = group // 2, lax.rem(group, 2)
        diagonals = jnp.zeros((16, TILE), F32)
        for k in range(PAIRS // 2):
            upper = root * OWN_TILES + half * (PAIRS // 2) + k
            signed = []
            for tile in (upper, upper + PAIRS):
                row = jnp.broadcast_to(sign[pl.ds(tile, 1), :], (TILE, TILE))
                block = cov_in[tile].astype(F32) * row * row.T
                diagonal = jnp.sum(jnp.where(iota(0) == iota(1), block, 0.0), axis=0, keepdims=True)
                w_rows = mask_weights(tile)
                w_wide = w_rows.astype(F32)
                carried = jnp.dot(w_rows, block.astype(BF16), preferred_element_type=F32)
                variance = jnp.sum(carried * w_wide, axis=1, keepdims=True)
                trace = jnp.sum(w_wide * w_wide * diagonal, axis=1, keepdims=True)
                linear = linear + jnp.where(lane == tile, variance, 0.0)
                linear = linear + jnp.where(lane == tile + 64, trace, 0.0)
                signed.append(block)
            diagonals = jnp.where(iota(0, (16, TILE)) == k, diagonal, diagonals)
            both = jnp.where(iota(0) <= iota(1), signed[0], signed[1])
            cov_out[root, half, k * TILE:(k + 1) * TILE, :] = both.astype(BF16)
        cov_out[root, half, PAIRS // 2 * TILE:, :] = diagonals.astype(BF16)
        return linear

    var_mine[...] = lax.fori_loop(0, 2 * COHORTS, cov_group, jnp.zeros((MASKS, TILE), F32))

    def to_cohorts(source, target, sent, received):
        return [
            pltpu.make_async_remote_copy(
                src_ref=source,
                dst_ref=target.at[step - 1],
                send_sem=sent.at[step - 1],
                recv_sem=received.at[step - 1],
                device_id={"cohort": cohort(step)},
                device_id_type=MESH,
            )
            for step in range(1, COHORTS)
        ]

    var_copies = to_cohorts(var_mine, var_got, var_send, var_recv)
    for copy in var_copies:
        copy.start()
    for way in range(2):
        cov_piece(way, 0).start()
        cov_piece(way, 1).start()

    load(1).wait()
    load(3).wait()

    def near(chunk, carry):
        for way in range(2):
            relative = 1 if way == 0 else 3

            def one(k, inner):
                rows = rows_of((1 - way) * HALF + chunk * CHUNK_TILES + k)
                buf[relative, rows, :] = buf[relative, rows, :] * factor_wide[rows, :]
                return inner

            lax.fori_loop(0, CHUNK_TILES, one, 0)
            piece(way, 1, chunk).start()
        return carry

    lax.fori_loop(0, CHUNKS, near, 0)

    for way in range(2):
        cov_piece(way, 0).wait_recv()
        root = cohort(1 if way == 0 else 3)
        cov_out[root, way] = (cov_out[root, way].astype(F32) + cov_got[0, way].astype(F32)).astype(BF16)
        cov_piece(way, 2).start()

    def onward(chunk, carry):
        for way in range(2):
            relative = 1 if way == 0 else 3
            piece(way, 0, chunk).wait_recv()

            def one(k, inner):
                rows = rows_of(way * HALF + chunk * CHUNK_TILES + k)
                landed = rows_of(chunk * CHUNK_TILES + k)
                term = buf[relative, rows, :].astype(F32) * factor_wide[rows, :].astype(F32)
                buf[relative, rows, :] = (term + got[0, way, landed, :].astype(F32)).astype(BF16)
                return inner

            lax.fori_loop(0, CHUNK_TILES, one, 0)
            piece(way, 2, chunk).start()
        return carry

    lax.fori_loop(0, CHUNKS, onward, 0)

    spreads = jnp.zeros((MASKS, TILE), F32)
    for half in range(2):
        cov_piece(1 - half, 1).wait_recv()
        cov_piece(half, 2).wait_recv()
        total = (
            cov_out[me, half].astype(F32)
            + cov_got[1, 1 - half].astype(F32)
            + cov_got[2, half].astype(F32)
        )
        for k in range(PAIRS // 2):
            square = total[k * TILE:(k + 1) * TILE, :]
            square = square * square
            row_at = PAIRS // 2 * TILE + k
            diagonal = total[row_at:row_at + 1, :]
            upper = jnp.where(iota(0) < iota(1), 2.0 * square, jnp.where(iota(0) == iota(1), square, 0.0))
            lower = jnp.where(iota(0) > iota(1), 2.0 * square, 0.0)
            first = me * OWN_TILES + half * (PAIRS // 2) + k
            for tile, part in ((first, upper), (first + PAIRS, lower)):
                w_wide = mask_weights(tile).astype(F32)
                w_square = w_wide * w_wide
                carried = jnp.dot(w_square, part, precision=HIGHEST, preferred_element_type=F32)
                if part is lower:
                    carried = carried + w_square * (diagonal * diagonal)
                spread = jnp.sum(carried * w_square, axis=1, keepdims=True)
                spreads = spreads + jnp.where(lane == tile, spread, 0.0)
    spread_mine[...] = spreads
    spread_copies = to_cohorts(spread_mine, spread_got, spread_send, spread_recv)
    for copy in spread_copies:
        copy.start()
    for copy in var_copies + spread_copies:
        copy.wait_recv()
    linear = var_mine[...] + var_got[0] + var_got[1] + var_got[2]
    spreads = spreads + spread_got[0] + spread_got[1] + spread_got[2]

    facts = jnp.concatenate(
        [
            jnp.where(lane < 64, linear, 0.0),
            spreads,
            jnp.broadcast_to(gene_row, (MASKS, TILE)),
            jnp.zeros((64 - 3 * MASKS, TILE), F32),
        ],
        axis=0,
    )
    slot_facts = lax.dot_general(
        slots, facts, (((1,), (1,)), ((), ())), precision=HIGHEST, preferred_element_type=F32
    )
    stats[...] = jnp.concatenate([slot_facts[:OWNERS], slot_facts[OWNERS:]], axis=1)
    stats_got[pl.ds(mine, 1), :] = stats[pl.ds(mine, 1), :]

    def send_stats(offset, carry):
        there = owner_at(offset)
        pltpu.make_async_remote_copy(
            src_ref=stats.at[pl.ds(there, 1)],
            dst_ref=stats_got.at[pl.ds(mine, 1)],
            send_sem=stat_send,
            recv_sem=stat_recv,
            device_id={"gene": there},
            device_id_type=MESH,
        ).start()
        return carry

    lax.fori_loop(1, OWNERS, send_stats, 0)

    load(0).wait()

    def finish(chunk, carry):
        for half in range(2):
            piece(1 - half, 1, chunk).wait_recv()
            piece(half, 2, chunk).wait_recv()

            def one(k, inner):
                tile = half * HALF + chunk * CHUNK_TILES + k
                rows = rows_of(tile)
                landed = rows_of(chunk * CHUNK_TILES + k)
                united = (
                    buf[0, rows, :].astype(F32) * factor_wide[rows, :].astype(F32)
                    + got[1, 1 - half, landed, :].astype(F32)
                    + got[2, half, landed, :].astype(F32)
                )
                w_rows = mask_weights(tile)
                burden = jnp.dot(w_rows, united.astype(BF16), preferred_element_type=F32)
                w_wide = w_rows.astype(F32)
                w_square = w_wide * w_wide
                w_high = w_square.astype(BF16).astype(F32)
                w_parts = jnp.concatenate([w_high, w_square - w_high], axis=0).astype(BF16)
                square = united * united
                high = square.astype(BF16)
                low = (square - high.astype(F32)).astype(BF16)
                main = jnp.dot(w_parts, high, preferred_element_type=F32)
                rest = jnp.dot(w_parts, low, preferred_element_type=F32)
                trace = jnp.sum(jnp.where(lane == tile + 64, linear, 0.0), axis=1, keepdims=True)
                total = main[:MASKS] + (main[MASKS:] + rest[:MASKS])
                first = pl.multiple_of(tile * 2 * MASKS, 2 * MASKS)
                held[pl.ds(first, MASKS), :] = burden
                held[pl.ds(first + MASKS, MASKS), :] = total - trace
                return inner

            lax.fori_loop(0, CHUNK_TILES, one, 0)
        return carry

    lax.fori_loop(0, CHUNKS, finish, 0)

    slots_narrow = slots.astype(BF16)
    for row in range(2 * MASKS):
        tiles = held[pl.ds(row, TILE, stride=2 * MASKS), :].astype(BF16)
        chosen = jnp.dot(slots_narrow, tiles, preferred_element_type=F32)
        for second in range(2):
            wide[pl.ds(second * 2 * MASKS + row, OWNERS, stride=4 * MASKS), :] = chosen[
                second * OWNERS:(second + 1) * OWNERS
            ]

    def narrow(index):
        first = pl.multiple_of(index * 4 * MASKS, 4 * MASKS)
        return wide[pl.ds(first, 4 * MASKS), :].astype(BF16)

    def send_slots(offset, carry):
        there = owner_at(offset)
        packed[there] = narrow(there)
        pltpu.make_async_remote_copy(
            src_ref=packed.at[there],
            dst_ref=arrived.at[mine],
            send_sem=pay_send,
            recv_sem=pay_recv,
            device_id={"gene": there},
            device_id_type=MESH,
        ).start()
        return carry

    lax.fori_loop(1, OWNERS, send_slots, 0)
    arrived[mine] = narrow(mine)

    pltpu.make_async_copy(stats_got.at[pl.ds(0, OWNERS - 1)], stats_got.at[pl.ds(0, OWNERS - 1)], stat_recv).wait()
    all_stats = stats_got[...]
    turned = jnp.concatenate([all_stats, jnp.zeros_like(all_stats)], axis=0).T
    gene_at = (iota(0, (GENES, OWNERS)) + 1).astype(F32)
    chosen_by = [
        (jnp.broadcast_to(turned[second * 64 + 2 * MASKS:second * 64 + 2 * MASKS + 1, :OWNERS], (GENES, OWNERS)) == gene_at)
        .astype(F32)
        for second in range(2)
    ]
    sums = [
        jnp.dot(chosen, all_stats, precision=HIGHEST, preferred_element_type=F32) for chosen in chosen_by
    ]
    moments = sums[0][:, :64] + sums[1][:, 64:]
    doubled = jnp.where(iota(1, (GENES, 64)) >= MASKS, 2.0 * moments, moments)
    scale = 1.0 / jnp.sqrt(jnp.maximum(doubled, 1.0))
    membership_of_gene = jnp.concatenate(chosen_by, axis=1).astype(BF16)

    pltpu.make_async_copy(arrived.at[pl.ds(0, OWNERS - 1)], arrived.at[pl.ds(0, OWNERS - 1)], pay_recv).wait()
    wide_got[...] = arrived[...].astype(F32).reshape(OWNERS * 4 * MASKS, TILE)
    for row in range(2 * MASKS):
        both = jnp.concatenate(
            [wide_got[pl.ds(second * 2 * MASKS + row, OWNERS, stride=4 * MASKS), :] for second in range(2)], axis=0
        ).astype(BF16)
        total = jnp.dot(membership_of_gene, both, preferred_element_type=F32)
        result = total * scale[:, row:row + 1]
        if row < MASKS:
            burden_out[:, row, :] = result
        else:
            skat_out[:, row - MASKS, :] = result

    def all_sent(chunk, carry):
        for way in range(2):
            for phase in range(3):
                piece(way, phase, chunk).wait_send()
        return carry

    lax.fori_loop(0, CHUNKS, all_sent, 0)
    for way in range(2):
        for phase in range(3):
            cov_piece(way, phase).wait_send()
    for copy in var_copies + spread_copies:
        copy.wait_send()
    pltpu.make_async_copy(stats.at[pl.ds(0, OWNERS - 1)], stats.at[pl.ds(0, OWNERS - 1)], stat_send).wait()
    pltpu.make_async_copy(packed.at[pl.ds(0, OWNERS - 1)], packed.at[pl.ds(0, OWNERS - 1)], pay_send).wait()


def shards(scores, flips, presence, covs, membership, weights, tile_owner, tile_gene):
    vmem = pl.BlockSpec(memory_space=pltpu.VMEM)
    hbm = pl.BlockSpec(memory_space=pl.ANY)
    out = jax.ShapeDtypeStruct((GENES, MASKS, TILE), F32)
    dma = pltpu.SemaphoreType.DMA
    scratch = [
        pltpu.VMEM((COHORTS, TILES * TILE, TILE), BF16),
        pltpu.VMEM((3, 2, HALF * TILE, TILE), BF16),
        pltpu.VMEM((TILES * TILE, TILE), BF16),
        pltpu.VMEM((TILES, TILE, TILE), BF16),
        pltpu.VMEM((COHORTS, 2, COV_ROWS, TILE), BF16),
        pltpu.VMEM((3, 2, COV_ROWS, TILE), BF16),
        pltpu.VMEM((TILES, TILE), F32),
        pltpu.VMEM((TILES, TILE), F32),
        pltpu.VMEM((TILE * 2 * MASKS, TILE), F32),
        pltpu.VMEM((MASKS, TILE), F32),
        pltpu.VMEM((COHORTS - 1, MASKS, TILE), F32),
        pltpu.VMEM((MASKS, TILE), F32),
        pltpu.VMEM((COHORTS - 1, MASKS, TILE), F32),
        pltpu.VMEM((OWNERS, TILE), F32),
        pltpu.VMEM((OWNERS, TILE), F32),
        pltpu.VMEM((OWNERS * 4 * MASKS, TILE), F32),
        pltpu.VMEM((OWNERS, 4 * MASKS, TILE), BF16),
        pltpu.VMEM((OWNERS, 4 * MASKS, TILE), BF16),
        pltpu.VMEM((OWNERS * 4 * MASKS, TILE), F32),
        dma((COHORTS,)),
        dma,
        dma((2, 3, CHUNKS)),
        dma((2, 3, CHUNKS)),
        dma((2, 3)),
        dma((2, 3)),
        dma((COHORTS - 1,)),
        dma((COHORTS - 1,)),
        dma((COHORTS - 1,)),
        dma((COHORTS - 1,)),
        dma,
        dma,
        dma,
        dma,
    ]
    return pl.pallas_call(
        kernel,
        out_shape=(out, out),
        in_specs=[hbm, vmem, vmem, hbm, vmem, vmem, vmem, vmem],
        out_specs=(vmem, vmem),
        scratch_shapes=scratch,
        compiler_params=pltpu.CompilerParams(
            collective_id=0, has_side_effects=True, vmem_limit_bytes=48 * 1024 * 1024
        ),
        cost_estimate=pl.CostEstimate(flops=500_000_000, bytes_accessed=9_000_000, transcendentals=0),
    )(
        scores,
        flips.reshape(TILES, TILE),
        presence.reshape(TILES, TILE),
        covs,
        membership,
        weights.reshape(TILES, TILE),
        tile_owner.reshape(1, TILES),
        tile_gene.reshape(1, TILES),
    )


def solution(mesh):
    return jax.shard_map(
        shards,
        mesh=mesh,
        in_specs=(
            P("cohort", "gene", None),
            P("cohort", "gene"),
            P("cohort", "gene"),
            P("cohort", "gene", None, None),
            P(None, "gene"),
            P("gene"),
            P("gene", None),
            P("gene"),
        ),
        out_specs=(P("gene", None, "cohort"), P("gene", None, "cohort")),
        check_vma=False,
    )
```

```python
import jax
import jax.numpy as jnp
from jax import lax
from jax.experimental import pallas as pl
from jax.experimental.pallas import tpu as pltpu
from jax.sharding import PartitionSpec as P

F32, BF16 = jnp.float32, jnp.bfloat16
MESH = pl.DeviceIdType.MESH
TILE = 128
TILES = 48
PAIRED = TILES // 2
HALF = TILE // 2
GROUP = PAIRED // 2
CHUNKS = 4
SQUARES = GROUP // CHUNKS
CHUNK_ROWS = SQUARES * TILE
COHORTS = 4
OWNERS = 64
SIDE = 8
BATCH = 4
AWAY = (0, 4, 3, 5, 2, 6, 1, 7)
GENES = 16
MASKS = 8
FIELDS = 2 * MASKS
OWN_TILES = TILES // COHORTS
PAIRS = OWN_TILES // 2
COV_ROWS = PAIRS // 2 * TILE + 16
FLIGHT = 3
SELECT = 32
HIGHEST = lax.Precision.HIGHEST


def rows_of(tile, count=1):
    return pl.ds(pl.multiple_of(tile * TILE, TILE), count * TILE)


def iota(axis, shape=(TILE, TILE)):
    return lax.broadcasted_iota(jnp.int32, shape, axis)


def swap(value):
    return pltpu.roll(value, HALF, 1)


def left(shape=(TILE, TILE)):
    return iota(1, shape) < HALF


def kernel(
    scores, flips_in, presence_in, covs, membership_in, weights_in, owner_in, gene_in,
    burden_out, skat_out,
    flips, presence, membership, weights, owner, gene,
    buf, got, factor_wide, cov_in, cov_out, cov_got, factor, sign, held,
    var_mine, var_got, spread_mine, spread_got, stats, stats_got,
    stats_relayed, stats_turned, wide, packed, relayed, arrived, wide_got,
    small_sem, far_sem, load_sem, cov_sem, send_sem, recv_sem, cov_send, cov_recv,
    var_send, var_recv, spread_send, spread_recv, stat_send, stat_recv, pay_send, pay_recv, relay_send, relay_recv,
):
    me = lax.axis_index("cohort")
    mine = lax.axis_index("gene")

    def cohort(relative):
        return lax.rem(me + relative, COHORTS)

    my_z = lax.rem(mine // 2, SIDE)
    my_place = 2 * (mine // 16) + lax.rem(mine, 2)

    def along_z(offset):
        return lax.rem(my_z + offset, SIDE)

    def across(offset):
        return lax.rem(my_place + offset, SIDE)

    def owner_of(z, place):
        return 16 * (place // 2) + 2 * z + lax.rem(place, 2)

    def columns(relative):
        return pl.ds(pl.multiple_of(cohort(relative) * TILE, TILE), TILE)

    def load(relative):
        return pltpu.make_async_copy(scores.at[0, :, columns(relative)], buf.at[relative], load_sem.at[relative])

    def load_far(group, chunk, second):
        rows = rows_of(second * PAIRED + group * GROUP + chunk * SQUARES, SQUARES)
        return pltpu.make_async_copy(
            scores.at[0, rows, columns(2)], buf.at[2, rows], far_sem.at[group, chunk, second]
        )

    pieces = ((flips_in, flips), (presence_in, presence), (membership_in, membership),
              (weights_in, weights), (owner_in, owner), (gene_in, gene))
    small = [pltpu.make_async_copy(source, target, small_sem.at[i]) for i, (source, target) in enumerate(pieces)]
    load_cov = pltpu.make_async_copy(covs.at[0], cov_in, cov_sem)
    small[0].start()
    small[1].start()
    for chunk in range(CHUNKS):
        for group in range(2):
            for second in range(2):
                load_far(group, chunk, second).start()

    barrier = pltpu.get_barrier_semaphore()
    for step in range(1, COHORTS):
        pl.semaphore_signal(barrier, inc=1, device_id={"cohort": cohort(step)}, device_id_type=MESH)

    for offset in range(1, SIDE):
        for there in (owner_of(along_z(offset), my_place), owner_of(my_z, across(offset))):
            pl.semaphore_signal(barrier, inc=1, device_id={"gene": there}, device_id_type=MESH)
    load(1).start()
    load(3).start()
    for copy in small[2:]:
        copy.start()
    load_cov.start()
    load(0).start()

    def piece(way, phase, part, chunk):
        group = 1 - way if phase == 1 else way
        relative = 2 if phase == 0 else (1 if way == 0 else 3)
        return pltpu.make_async_remote_copy(
            src_ref=buf.at[relative, rows_of(part * PAIRED + group * GROUP + chunk * SQUARES, SQUARES)],
            dst_ref=got.at[phase, way, rows_of(part * GROUP + chunk * SQUARES, SQUARES)],
            send_sem=send_sem.at[way, phase, part, chunk],
            recv_sem=recv_sem.at[way, phase, part, chunk],
            device_id={"cohort": cohort(1 if way == 0 else 3)},
            device_id_type=MESH,
        )

    def cov_piece(way, phase):
        half = 1 - way if phase == 1 else way
        relative = 2 if phase == 0 else (1 if way == 0 else 3)
        return pltpu.make_async_remote_copy(
            src_ref=cov_out.at[cohort(relative), half],
            dst_ref=cov_got.at[phase, way],
            send_sem=cov_send.at[way, phase],
            recv_sem=cov_recv.at[way, phase],
            device_id={"cohort": cohort(1 if way == 0 else 3)},
            device_id_type=MESH,
        )

    def pair_up(relative, square):
        first, second = rows_of(square), rows_of(square + PAIRED)
        x = buf[relative, first, :].astype(F32)
        y = buf[relative, second, :].astype(F32)
        sign_of = factor_wide[first, :].astype(F32)
        buf[relative, first, :] = (jnp.where(left(), x, swap(y)) * sign_of).astype(BF16)
        buf[relative, second, :] = (jnp.where(left(), swap(x), y) * sign_of).astype(BF16)

    def mask_weights(tile):
        member = membership[:, rows_of(tile)].astype(F32)
        return (weights[pl.ds(tile, 1), :] * (1.0 + 3.0 * member) / 4.0).astype(BF16)

    small[0].wait()
    small[1].wait()
    sign[...] = 1.0 - 2.0 * flips[...].astype(F32)
    factor[...] = sign[...] * presence[...].astype(F32)

    def far(group, chunk):
        load_far(group, chunk, 0).wait()
        load_far(group, chunk, 1).wait()

        def one(k, inner):
            square = group * GROUP + chunk * SQUARES + k
            x = jnp.broadcast_to(factor[pl.ds(square, 1), :], (TILE, TILE)).T
            y = jnp.broadcast_to(factor[pl.ds(square + PAIRED, 1), :], (TILE, TILE)).T
            factor_wide[rows_of(square), :] = jnp.where(left(), x, y).astype(BF16)
            pair_up(2, square)
            return inner

        lax.fori_loop(0, SQUARES, one, 0, unroll=True)

    far(0, 0)
    far(1, 0)
    pl.semaphore_wait(barrier, 2 * (SIDE - 1) + COHORTS - 1)
    piece(0, 0, 0, 0).start()
    piece(1, 0, 0, 0).start()

    def more_far(chunk, carry):
        for way in range(2):
            far(way, chunk)
            piece(way, 0, 0, chunk).start()
        return carry

    lax.fori_loop(1, CHUNKS, more_far, 0)

    for copy in small[2:]:
        copy.wait()
    load_cov.wait()
    lane = iota(1, (MASKS, TILE))

    def cov_group(group, linear):
        root, half = group // 2, lax.rem(group, 2)
        diagonals = jnp.zeros((16, TILE), F32)
        for k in range(PAIRS // 2):
            upper = root * OWN_TILES + half * (PAIRS // 2) + k
            signed = []
            for tile in (upper, upper + PAIRS):
                row = jnp.broadcast_to(sign[pl.ds(tile, 1), :], (TILE, TILE))
                block = cov_in[tile].astype(F32) * row * row.T
                diagonal = jnp.sum(jnp.where(iota(0) == iota(1), block, 0.0), axis=0, keepdims=True)
                w_rows = mask_weights(tile)
                w_wide = w_rows.astype(F32)
                carried = jnp.dot(w_rows, block.astype(BF16), preferred_element_type=F32)
                variance = jnp.sum(carried * w_wide, axis=1, keepdims=True)
                trace = jnp.sum(w_wide * w_wide * diagonal, axis=1, keepdims=True)
                linear = linear + jnp.where(lane == tile, variance, 0.0)
                linear = linear + jnp.where(lane == tile + 64, trace, 0.0)
                signed.append(block)
            diagonals = jnp.where(iota(0, (16, TILE)) == k, diagonal, diagonals)
            both = jnp.where(iota(0) <= iota(1), signed[0], signed[1])
            cov_out[root, half, k * TILE:(k + 1) * TILE, :] = both.astype(BF16)
        cov_out[root, half, PAIRS // 2 * TILE:, :] = diagonals.astype(BF16)
        return linear

    var_mine[...] = lax.fori_loop(0, 2 * COHORTS, cov_group, jnp.zeros((MASKS, TILE), F32))

    def to_cohorts(source, target, sent, received):
        return [
            pltpu.make_async_remote_copy(
                src_ref=source,
                dst_ref=target.at[step - 1],
                send_sem=sent.at[step - 1],
                recv_sem=received.at[step - 1],
                device_id={"cohort": cohort(step)},
                device_id_type=MESH,
            )
            for step in range(1, COHORTS)
        ]

    var_copies = to_cohorts(var_mine, var_got, var_send, var_recv)
    for copy in var_copies:
        copy.start()

    chunks = range(CHUNKS)
    order = [(0, 0, c) for c in chunks] + [(1, 0, c) for c in chunks] + [(0, None, 0), (1, None, 0)]
    order += [(2, 0, c) for c in chunks] + [(2, None, 0)]
    order += [(phase, 1, c) for phase in range(3) for c in chunks]

    def copy_of(item, way):
        phase, part, chunk = item
        return cov_piece(way, phase) if part is None else piece(way, phase, part, chunk)

    def prepare(item, way):
        phase, part, chunk = item
        relative = 1 if way == 0 else 3
        if part is None and phase == 2:
            cov_piece(way, 0).wait_recv()
            root = cohort(relative)
            cov_out[root, way] = (cov_out[root, way].astype(F32) + cov_got[0, way].astype(F32)).astype(BF16)
        elif part == 0 and phase == 1:
            for k in range(SQUARES):
                pair_up(relative, (1 - way) * GROUP + chunk * SQUARES + k)
        elif part is not None and phase == 2:
            piece(way, 0, part, chunk).wait_recv()
            for k in range(SQUARES):
                rows = rows_of(part * PAIRED + way * GROUP + chunk * SQUARES + k)
                landed = rows_of(part * GROUP + chunk * SQUARES + k)
                if part == 0:
                    pair_up(relative, way * GROUP + chunk * SQUARES + k)
                total = buf[relative, rows, :].astype(F32) + got[0, way, landed, :].astype(F32)
                buf[relative, rows, :] = total.astype(BF16)

    def send_up_to(first, end):
        for index in range(first, end):
            for way in range(2):
                prepare(order[index], way)
                copy_of(order[index - FLIGHT], way).wait_send()
                copy_of(order[index], way).start()

    load(1).wait()
    load(3).wait()
    for item in order[:CHUNKS - FLIGHT]:
        for way in range(2):
            copy_of(item, way).wait_send()
    send_up_to(CHUNKS, 17)

    padding = jnp.full((1, TILE - TILES), -1.0, F32)
    owner_row = jnp.concatenate([owner[...].astype(F32), padding], axis=1)
    gene_row = jnp.concatenate([gene[...].astype(F32), padding], axis=1) + 1.0
    owner_rows = jnp.broadcast_to(owner_row, (TILE, TILE))
    same = (owner_rows == owner_rows.T) & (iota(0) < iota(1))
    rank_row = jnp.sum(same.astype(F32), axis=0, keepdims=True)
    owner_int = owner[...]
    place_int = 8 * ((owner_int >> 1) & 7) + 2 * (owner_int >> 4) + (owner_int & 1)
    place_row = jnp.concatenate([place_int.astype(F32), padding], axis=1)
    slot_row = jnp.where(place_row >= 0.0, place_row + OWNERS * rank_row, -1.0)
    slots = (slot_row == iota(0).astype(F32)).astype(F32)
    selector = jnp.concatenate(
        [slots[:, :SELECT], pltpu.roll(slots, TILE - PAIRED, 1)[:, :SELECT]], axis=0
    ).astype(BF16)

    load(0).wait()

    def own(index, carry):
        for group in range(2):
            pair_up(0, group * GROUP + index)
        return carry

    lax.fori_loop(0, GROUP, own, 0)

    for copy in var_copies:
        copy.wait_recv()
    linear = var_mine[...] + var_got[0] + var_got[1] + var_got[2]
    held[pl.ds(PAIRED * FIELDS, (SELECT - PAIRED) * FIELDS), :] = jnp.zeros(
        ((SELECT - PAIRED) * FIELDS, TILE), F32
    )

    def by_half(rows, count):
        parts = [rows[i * MASKS:(i + 1) * MASKS] for i in range(count)]
        return [jnp.where(left((MASKS, TILE)), parts[i], parts[i + 1]) for i in range(0, count, 2)]

    def finish(part):
        def step(chunk, carry):
            for group in range(2):
                piece(1 - group, 1, part, chunk).wait_recv()
                piece(group, 2, part, chunk).wait_recv()

                def one(k, inner):
                    square = group * GROUP + chunk * SQUARES + k
                    landed = rows_of(part * GROUP + chunk * SQUARES + k)
                    united = (
                        buf[0, rows_of(part * PAIRED + square), :].astype(F32)
                        + got[1, 1 - group, landed, :].astype(F32)
                        + got[2, group, landed, :].astype(F32)
                    )
                    w_wide = jnp.concatenate([mask_weights(square), mask_weights(square + PAIRED)], axis=0).astype(F32)
                    w_square = w_wide * w_wide
                    w_high = w_square.astype(BF16).astype(F32)
                    w_parts = jnp.concatenate([w_high, w_square - w_high], axis=0).astype(BF16)
                    squared = united * united
                    high = squared.astype(BF16)
                    low = (squared - high.astype(F32)).astype(BF16)
                    (burden,) = by_half(
                        jnp.dot(w_wide.astype(BF16), united.astype(BF16), preferred_element_type=F32), 2
                    )
                    main = by_half(jnp.dot(w_parts, high, preferred_element_type=F32), 4)
                    rest = by_half(jnp.dot(w_parts, low, preferred_element_type=F32), 4)
                    trace = [
                        jnp.sum(jnp.where(lane == tile + 64, linear, 0.0), axis=1, keepdims=True)
                        for tile in (square, square + PAIRED)
                    ]
                    traces = jnp.where(left((MASKS, TILE)), trace[0], trace[1])
                    first = pl.multiple_of(square * FIELDS, FIELDS)
                    held[pl.ds(first, MASKS), :] = burden
                    held[pl.ds(first + MASKS, MASKS), :] = main[0] + (main[1] + rest[0]) - traces
                    return inner

                lax.fori_loop(0, SQUARES, one, 0, unroll=True)
            return carry

        lax.fori_loop(0, CHUNKS, step, 0)

    def payload(part):
        for row in range(FIELDS):
            tiles = held[pl.ds(row, SELECT, stride=FIELDS), :].astype(BF16)
            chosen = jnp.dot(selector, tiles, preferred_element_type=F32)
            near_tiles, far_tiles = chosen[:TILE], chosen[TILE:]
            wide[pl.ds(row, OWNERS, stride=FIELDS), :] = jnp.where(
                left((OWNERS, TILE)),
                near_tiles[:OWNERS] + swap(far_tiles[:OWNERS]),
                swap(near_tiles[OWNERS:]) + far_tiles[OWNERS:],
            )
        packed[part] = wide[...].astype(BF16).reshape(SIDE, SIDE, FIELDS, TILE)
        for k in range(1, SIDE):
            first_stage(part, k).start()
        relayed[part, 0] = packed[part, my_z]

    def first_stage(part, k):
        there = along_z(AWAY[k])
        return pltpu.make_async_remote_copy(
            src_ref=packed.at[part, there],
            dst_ref=relayed.at[part, k],
            send_sem=pay_send.at[part, k],
            recv_sem=pay_recv.at[part, k],
            device_id={"gene": owner_of(there, my_place)},
            device_id_type=MESH,
        )

    def second_stage(part, batch, k):
        there = across(k)
        rows = pl.ds(batch * BATCH, BATCH)
        return pltpu.make_async_remote_copy(
            src_ref=relayed.at[part, rows, there],
            dst_ref=arrived.at[part, k, rows],
            send_sem=relay_send.at[part, batch, k],
            recv_sem=relay_recv.at[part, batch, k],
            device_id={"gene": owner_of(my_z, there)},
            device_id_type=MESH,
        )

    def relay(part):
        for batch in range(SIDE // BATCH):
            for k in range(max(1, batch * BATCH), (batch + 1) * BATCH):
                first_stage(part, k).wait_recv()
            for k in range(1, SIDE):
                second_stage(part, batch, k).start()
            rows = slice(batch * BATCH, (batch + 1) * BATCH)
            arrived[part, 0, rows] = relayed[part, rows, my_place]

    finish(0)
    payload(0)
    send_up_to(17, 19)

    spreads = jnp.zeros((MASKS, TILE), F32)
    for half in range(2):
        cov_piece(1 - half, 1).wait_recv()
        cov_piece(half, 2).wait_recv()
        total = (
            cov_out[me, half].astype(F32)
            + cov_got[1, 1 - half].astype(F32)
            + cov_got[2, half].astype(F32)
        )
        for k in range(PAIRS // 2):
            square = total[k * TILE:(k + 1) * TILE, :]
            square = square * square
            row_at = PAIRS // 2 * TILE + k
            diagonal = total[row_at:row_at + 1, :]
            upper = jnp.where(iota(0) < iota(1), 2.0 * square, jnp.where(iota(0) == iota(1), square, 0.0))
            lower = jnp.where(iota(0) > iota(1), 2.0 * square, 0.0)
            first = me * OWN_TILES + half * (PAIRS // 2) + k
            for tile, part in ((first, upper), (first + PAIRS, lower)):
                w_wide = mask_weights(tile).astype(F32)
                w_square = w_wide * w_wide
                carried = jnp.dot(w_square, part, precision=HIGHEST, preferred_element_type=F32)
                if part is lower:
                    carried = carried + w_square * (diagonal * diagonal)
                spread = jnp.sum(carried * w_square, axis=1, keepdims=True)
                spreads = spreads + jnp.where(lane == tile, spread, 0.0)
    spread_mine[...] = spreads
    spread_copies = to_cohorts(spread_mine, spread_got, spread_send, spread_recv)
    for copy in spread_copies:
        copy.start()
    send_up_to(19, 20)
    relay(0)
    send_up_to(20, 21)
    for copy in spread_copies:
        copy.wait_recv()
    spreads = spreads + spread_got[0] + spread_got[1] + spread_got[2]

    facts = jnp.concatenate(
        [
            jnp.where(lane < 64, linear, 0.0),
            spreads,
            jnp.broadcast_to(gene_row, (MASKS, TILE)),
            jnp.zeros((64 - 3 * MASKS, TILE), F32),
        ],
        axis=0,
    )
    slot_facts = lax.dot_general(
        slots, facts, (((1,), (1,)), ((), ())), precision=HIGHEST, preferred_element_type=F32
    )
    stats[...] = jnp.concatenate([slot_facts[:OWNERS], slot_facts[OWNERS:]], axis=1).reshape(SIDE, SIDE, TILE)

    def first_stats(k):
        there = along_z(AWAY[k])
        return pltpu.make_async_remote_copy(
            src_ref=stats.at[there],
            dst_ref=stats_relayed.at[k],
            send_sem=stat_send.at[0, k],
            recv_sem=stat_recv.at[0, k],
            device_id={"gene": owner_of(there, my_place)},
            device_id_type=MESH,
        )

    def second_stats(k):
        there = across(k)
        return pltpu.make_async_remote_copy(
            src_ref=stats_turned.at[there],
            dst_ref=stats_got.at[k],
            send_sem=stat_send.at[1, k],
            recv_sem=stat_recv.at[1, k],
            device_id={"gene": owner_of(my_z, there)},
            device_id_type=MESH,
        )

    for k in range(1, SIDE):
        first_stats(k).start()
    stats_relayed[0] = stats[my_z]
    send_up_to(21, 22)
    for k in range(1, SIDE):
        first_stats(k).wait_recv()
    for place in range(SIDE):
        stats_turned[place] = stats_relayed[:, place, :]
    for k in range(1, SIDE):
        second_stats(k).start()
    stats_got[0] = stats_turned[my_place]

    send_up_to(22, len(order))
    finish(1)
    payload(1)

    for k in range(1, SIDE):
        second_stats(k).wait_recv()
    all_stats = stats_got[...].reshape(OWNERS, TILE)
    turned = jnp.concatenate([all_stats, jnp.zeros_like(all_stats)], axis=0).T
    gene_at = (iota(0, (GENES, OWNERS)) + 1).astype(F32)
    chosen_by = jnp.concatenate(
        [
            jnp.where(
                jnp.broadcast_to(turned[row:row + 1, :OWNERS], (GENES, OWNERS)) == gene_at, 1.0, 0.0
            )
            for row in (FIELDS, 64 + FIELDS)
        ],
        axis=0,
    )
    sums = jnp.dot(chosen_by, all_stats, precision=HIGHEST, preferred_element_type=F32)
    moments = sums[:GENES, :64] + sums[GENES:, 64:]
    doubled = jnp.where(iota(1, (GENES, 64)) >= MASKS, 2.0 * moments, moments)
    scale = 1.0 / jnp.sqrt(jnp.maximum(doubled, 1.0))
    chosen_by = chosen_by.astype(BF16)

    def gather(part):
        for batch in range(SIDE // BATCH):
            for k in range(1, SIDE):
                second_stage(part, batch, k).wait_recv()
        wide_got[...] = arrived[part].astype(F32).reshape(OWNERS * FIELDS, TILE)
        results = []
        for row in range(FIELDS):
            received = wide_got[pl.ds(row, OWNERS, stride=FIELDS), :].astype(BF16)
            both = jnp.dot(chosen_by, received, preferred_element_type=F32)
            if part == 0:
                total = both[:GENES] + swap(both[GENES:])
            else:
                total = swap(both[:GENES]) + both[GENES:]
            results.append(total * scale[:, row:row + 1])
        return results

    firsts = gather(0)
    for row in range(FIELDS):
        target = burden_out if row < MASKS else skat_out
        target[:, row % MASKS, :] = firsts[row]

    relay(1)
    seconds = gather(1)
    for row in range(FIELDS):
        target = burden_out if row < MASKS else skat_out
        target[:, row % MASKS, :] = jnp.where(left((GENES, TILE)), target[:, row % MASKS, :], seconds[row])

    for item in order[-FLIGHT:]:
        for way in range(2):
            copy_of(item, way).wait_send()
    for copy in var_copies + spread_copies:
        copy.wait_send()
    for k in range(1, SIDE):
        first_stats(k).wait_send()
        second_stats(k).wait_send()
        for part in range(2):
            first_stage(part, k).wait_send()
            for batch in range(SIDE // BATCH):
                second_stage(part, batch, k).wait_send()


def shards(scores, flips, presence, covs, membership, weights, tile_owner, tile_gene):
    vmem = pl.BlockSpec(memory_space=pltpu.VMEM)
    hbm = pl.BlockSpec(memory_space=pl.ANY)
    out = jax.ShapeDtypeStruct((GENES, MASKS, TILE), F32)
    dma = pltpu.SemaphoreType.DMA
    I32 = jnp.int32
    scratch = [
        pltpu.VMEM((TILES, TILE), I32),
        pltpu.VMEM((TILES, TILE), I32),
        pltpu.VMEM((MASKS, TILES * TILE), I32),
        pltpu.VMEM((TILES, TILE), F32),
        pltpu.VMEM((1, TILES), I32),
        pltpu.VMEM((1, TILES), I32),
        pltpu.VMEM((COHORTS, TILES * TILE, TILE), BF16),
        pltpu.VMEM((3, 2, 2 * GROUP * TILE, TILE), BF16),
        pltpu.VMEM((PAIRED * TILE, TILE), BF16),
        pltpu.VMEM((TILES, TILE, TILE), BF16),
        pltpu.VMEM((COHORTS, 2, COV_ROWS, TILE), BF16),
        pltpu.VMEM((3, 2, COV_ROWS, TILE), BF16),
        pltpu.VMEM((TILES, TILE), F32),
        pltpu.VMEM((TILES, TILE), F32),
        pltpu.VMEM((SELECT * FIELDS, TILE), F32),
        pltpu.VMEM((MASKS, TILE), F32),
        pltpu.VMEM((COHORTS - 1, MASKS, TILE), F32),
        pltpu.VMEM((MASKS, TILE), F32),
        pltpu.VMEM((COHORTS - 1, MASKS, TILE), F32),
        pltpu.VMEM((SIDE, SIDE, TILE), F32),
        pltpu.VMEM((SIDE, SIDE, TILE), F32),
        pltpu.VMEM((SIDE, SIDE, TILE), F32),
        pltpu.VMEM((SIDE, SIDE, TILE), F32),
        pltpu.VMEM((OWNERS * FIELDS, TILE), F32),
        pltpu.VMEM((2, SIDE, SIDE, FIELDS, TILE), BF16),
        pltpu.VMEM((2, SIDE, SIDE, FIELDS, TILE), BF16),
        pltpu.VMEM((2, SIDE, SIDE, FIELDS, TILE), BF16),
        pltpu.VMEM((OWNERS * FIELDS, TILE), F32),
        dma((6,)),
        dma((2, CHUNKS, 2)),
        dma((COHORTS,)),
        dma,
        dma((2, 3, 2, CHUNKS)),
        dma((2, 3, 2, CHUNKS)),
        dma((2, 3)),
        dma((2, 3)),
        dma((COHORTS - 1,)),
        dma((COHORTS - 1,)),
        dma((COHORTS - 1,)),
        dma((COHORTS - 1,)),
        dma((2, SIDE)),
        dma((2, SIDE)),
        dma((2, SIDE)),
        dma((2, SIDE)),
        dma((2, SIDE // BATCH, SIDE)),
        dma((2, SIDE // BATCH, SIDE)),
    ]
    return pl.pallas_call(
        kernel,
        out_shape=(out, out),
        in_specs=[hbm] * 8,
        out_specs=(vmem, vmem),
        scratch_shapes=scratch,
        compiler_params=pltpu.CompilerParams(
            collective_id=0, has_side_effects=True, vmem_limit_bytes=48 * 1024 * 1024
        ),
        cost_estimate=pl.CostEstimate(flops=500_000_000, bytes_accessed=9_000_000, transcendentals=0),
    )(
        scores,
        flips.reshape(TILES, TILE),
        presence.reshape(TILES, TILE),
        covs,
        membership,
        weights.reshape(TILES, TILE),
        tile_owner.reshape(1, TILES),
        tile_gene.reshape(1, TILES),
    )


def solution(mesh):
    return jax.shard_map(
        shards,
        mesh=mesh,
        in_specs=(
            P("cohort", "gene", None),
            P("cohort", "gene"),
            P("cohort", "gene"),
            P("cohort", "gene", None, None),
            P(None, "gene"),
            P("gene"),
            P("gene", None),
            P("gene"),
        ),
        out_specs=(P("gene", None, "cohort"), P("gene", None, "cohort")),
        check_vma=False,
    )
```

```python
import jax
import jax.numpy as jnp
from jax import lax
from jax.experimental import pallas as pl
from jax.experimental.pallas import tpu as pltpu
from jax.sharding import PartitionSpec as P

F32, BF16 = jnp.float32, jnp.bfloat16
MESH = pl.DeviceIdType.MESH
TILE = 128
TILES = 48
PAIRED = TILES // 2
HALF = TILE // 2
GROUP = PAIRED // 2
CHUNKS = 4
SQUARES = GROUP // CHUNKS
CHUNK_ROWS = SQUARES * TILE
COHORTS = 4
OWNERS = 64
SIDE = 8
BATCH = 4
AWAY = (0, 4, 3, 5, 2, 6, 1, 7)
GENES = 16
MASKS = 8
FIELDS = 2 * MASKS
OWN_TILES = TILES // COHORTS
PAIRS = OWN_TILES // 2
COV_ROWS = PAIRS // 2 * TILE + 16
FLIGHT = 3
SELECT = 32
HIGHEST = lax.Precision.HIGHEST


def rows_of(tile, count=1):
    return pl.ds(pl.multiple_of(tile * TILE, TILE), count * TILE)


def iota(axis, shape=(TILE, TILE)):
    return lax.broadcasted_iota(jnp.int32, shape, axis)


def swap(value):
    return pltpu.roll(value, HALF, 1)


def left(shape=(TILE, TILE)):
    return iota(1, shape) < HALF


def kernel(
    scores, flips_in, presence_in, covs, membership_in, weights_in, owner_in, gene_in,
    burden_out, skat_out,
    flips, presence, membership, weights, owner, gene,
    buf, got, factor_wide, cov_in, cov_out, cov_got, factor, sign, held,
    var_mine, var_got, spread_mine, spread_got, stats, stats_got,
    stats_relayed, stats_turned, wide, packed, relayed, arrived, wide_got,
    small_sem, far_sem, load_sem, cov_sem, send_sem, recv_sem, cov_send, cov_recv,
    var_send, var_recv, spread_send, spread_recv, stat_send, stat_recv, pay_send, pay_recv, relay_send, relay_recv,
):
    me = lax.axis_index("cohort")
    mine = lax.axis_index("gene")

    def cohort(relative):
        return lax.rem(me + relative, COHORTS)

    my_z = lax.rem(mine // 2, SIDE)
    my_place = 2 * (mine // 16) + lax.rem(mine, 2)

    def along_z(offset):
        return lax.rem(my_z + offset, SIDE)

    def across(offset):
        return lax.rem(my_place + offset, SIDE)

    def owner_of(z, place):
        return 16 * (place // 2) + 2 * z + lax.rem(place, 2)

    def columns(relative):
        return pl.ds(pl.multiple_of(cohort(relative) * TILE, TILE), TILE)

    def load(relative):
        return pltpu.make_async_copy(scores.at[0, :, columns(relative)], buf.at[relative], load_sem.at[relative])

    def load_far(group, chunk, second):
        rows = rows_of(second * PAIRED + group * GROUP + chunk * SQUARES, SQUARES)
        return pltpu.make_async_copy(
            scores.at[0, rows, columns(2)], buf.at[2, rows], far_sem.at[group, chunk, second]
        )

    pieces = ((flips_in, flips), (presence_in, presence), (membership_in, membership),
              (weights_in, weights), (owner_in, owner), (gene_in, gene))
    small = [pltpu.make_async_copy(source, target, small_sem.at[i]) for i, (source, target) in enumerate(pieces)]
    load_cov = pltpu.make_async_copy(covs.at[0], cov_in, cov_sem)
    barrier = pltpu.get_barrier_semaphore()
    for step in range(1, COHORTS):
        pl.semaphore_signal(barrier, inc=1, device_id={"cohort": cohort(step)}, device_id_type=MESH)

    for offset in range(1, SIDE):
        for there in (owner_of(along_z(offset), my_place), owner_of(my_z, across(offset))):
            pl.semaphore_signal(barrier, inc=1, device_id={"gene": there}, device_id_type=MESH)
    small[0].start()
    small[1].start()
    for chunk in range(CHUNKS):
        for group in range(2):
            for second in range(2):
                load_far(group, chunk, second).start()

    load(1).start()
    load(3).start()
    for copy in small[2:]:
        copy.start()
    load_cov.start()
    load(0).start()

    def piece(way, phase, part, chunk):
        group = 1 - way if phase == 1 else way
        relative = 2 if phase == 0 else (1 if way == 0 else 3)
        return pltpu.make_async_remote_copy(
            src_ref=buf.at[relative, rows_of(part * PAIRED + group * GROUP + chunk * SQUARES, SQUARES)],
            dst_ref=got.at[phase, way, rows_of(part * GROUP + chunk * SQUARES, SQUARES)],
            send_sem=send_sem.at[way, phase, part, chunk],
            recv_sem=recv_sem.at[way, phase, part, chunk],
            device_id={"cohort": cohort(1 if way == 0 else 3)},
            device_id_type=MESH,
        )

    def cov_piece(way, phase):
        half = 1 - way if phase == 1 else way
        relative = 2 if phase == 0 else (1 if way == 0 else 3)
        return pltpu.make_async_remote_copy(
            src_ref=cov_out.at[cohort(relative), half],
            dst_ref=cov_got.at[phase, way],
            send_sem=cov_send.at[way, phase],
            recv_sem=cov_recv.at[way, phase],
            device_id={"cohort": cohort(1 if way == 0 else 3)},
            device_id_type=MESH,
        )

    def pair_up(relative, square):
        first, second = rows_of(square), rows_of(square + PAIRED)
        x = buf[relative, first, :].astype(F32)
        y = buf[relative, second, :].astype(F32)
        sign_of = factor_wide[first, :].astype(F32)
        buf[relative, first, :] = (jnp.where(left(), x, swap(y)) * sign_of).astype(BF16)
        buf[relative, second, :] = (jnp.where(left(), swap(x), y) * sign_of).astype(BF16)

    def mask_weights(tile):
        member = membership[:, rows_of(tile)].astype(F32)
        return (weights[pl.ds(tile, 1), :] * (1.0 + 3.0 * member) / 4.0).astype(BF16)

    small[0].wait()
    small[1].wait()
    sign[...] = 1.0 - 2.0 * flips[...].astype(F32)
    factor[...] = sign[...] * presence[...].astype(F32)

    def far(group, chunk):
        load_far(group, chunk, 0).wait()
        load_far(group, chunk, 1).wait()

        def one(k, inner):
            square = group * GROUP + chunk * SQUARES + k
            x = jnp.broadcast_to(factor[pl.ds(square, 1), :], (TILE, TILE)).T
            y = jnp.broadcast_to(factor[pl.ds(square + PAIRED, 1), :], (TILE, TILE)).T
            factor_wide[rows_of(square), :] = jnp.where(left(), x, y).astype(BF16)
            pair_up(2, square)
            return inner

        lax.fori_loop(0, SQUARES, one, 0, unroll=True)

    far(0, 0)
    far(1, 0)
    pl.semaphore_wait(barrier, 2 * (SIDE - 1) + COHORTS - 1)
    piece(0, 0, 0, 0).start()
    piece(1, 0, 0, 0).start()

    def more_far(chunk, carry):
        for way in range(2):
            far(way, chunk)
            piece(way, 0, 0, chunk).start()
        return carry

    lax.fori_loop(1, CHUNKS, more_far, 0)

    for copy in small[2:]:
        copy.wait()
    load_cov.wait()
    lane = iota(1, (MASKS, TILE))

    def cov_group(group, linear):
        root, half = group // 2, lax.rem(group, 2)
        diagonals = jnp.zeros((16, TILE), F32)
        for k in range(PAIRS // 2):
            upper = root * OWN_TILES + half * (PAIRS // 2) + k
            signed = []
            for tile in (upper, upper + PAIRS):
                row = jnp.broadcast_to(sign[pl.ds(tile, 1), :], (TILE, TILE))
                block = cov_in[tile].astype(F32) * row * row.T
                diagonal = jnp.sum(jnp.where(iota(0) == iota(1), block, 0.0), axis=0, keepdims=True)
                w_rows = mask_weights(tile)
                w_wide = w_rows.astype(F32)
                carried = jnp.dot(w_rows, block.astype(BF16), preferred_element_type=F32)
                variance = jnp.sum(carried * w_wide, axis=1, keepdims=True)
                trace = jnp.sum(w_wide * w_wide * diagonal, axis=1, keepdims=True)
                linear = linear + jnp.where(lane == tile, variance, 0.0)
                linear = linear + jnp.where(lane == tile + 64, trace, 0.0)
                signed.append(block)
            diagonals = jnp.where(iota(0, (16, TILE)) == k, diagonal, diagonals)
            both = jnp.where(iota(0) <= iota(1), signed[0], signed[1])
            cov_out[root, half, k * TILE:(k + 1) * TILE, :] = both.astype(BF16)
        cov_out[root, half, PAIRS // 2 * TILE:, :] = diagonals.astype(BF16)
        return linear

    var_mine[...] = lax.fori_loop(0, 2 * COHORTS, cov_group, jnp.zeros((MASKS, TILE), F32))

    def to_cohorts(source, target, sent, received):
        return [
            pltpu.make_async_remote_copy(
                src_ref=source,
                dst_ref=target.at[step - 1],
                send_sem=sent.at[step - 1],
                recv_sem=received.at[step - 1],
                device_id={"cohort": cohort(step)},
                device_id_type=MESH,
            )
            for step in range(1, COHORTS)
        ]

    var_copies = to_cohorts(var_mine, var_got, var_send, var_recv)
    for copy in var_copies:
        copy.start()

    chunks = range(CHUNKS)
    order = [(0, 0, c) for c in chunks] + [(1, 0, c) for c in chunks] + [(0, None, 0), (1, None, 0)]
    order += [(2, 0, c) for c in chunks] + [(2, None, 0)]
    order += [(phase, 1, c) for phase in range(3) for c in chunks]

    def copy_of(item, way):
        phase, part, chunk = item
        return cov_piece(way, phase) if part is None else piece(way, phase, part, chunk)

    def prepare(item, way):
        phase, part, chunk = item
        relative = 1 if way == 0 else 3
        if part is None and phase == 2:
            cov_piece(way, 0).wait_recv()
            root = cohort(relative)
            cov_out[root, way] = (cov_out[root, way].astype(F32) + cov_got[0, way].astype(F32)).astype(BF16)
        elif part == 0 and phase == 1:
            for k in range(SQUARES):
                pair_up(relative, (1 - way) * GROUP + chunk * SQUARES + k)
        elif part is not None and phase == 2:
            piece(way, 0, part, chunk).wait_recv()
            for k in range(SQUARES):
                rows = rows_of(part * PAIRED + way * GROUP + chunk * SQUARES + k)
                landed = rows_of(part * GROUP + chunk * SQUARES + k)
                if part == 0:
                    pair_up(relative, way * GROUP + chunk * SQUARES + k)
                total = buf[relative, rows, :].astype(F32) + got[0, way, landed, :].astype(F32)
                buf[relative, rows, :] = total.astype(BF16)

    def send_up_to(first, end):
        for index in range(first, end):
            for way in range(2):
                prepare(order[index], way)
                copy_of(order[index - FLIGHT], way).wait_send()
                copy_of(order[index], way).start()

    load(1).wait()
    load(3).wait()
    for item in order[:CHUNKS - FLIGHT]:
        for way in range(2):
            copy_of(item, way).wait_send()
    send_up_to(CHUNKS, 17)

    padding = jnp.full((1, TILE - TILES), -1.0, F32)
    owner_row = jnp.concatenate([owner[...].astype(F32), padding], axis=1)
    gene_row = jnp.concatenate([gene[...].astype(F32), padding], axis=1) + 1.0
    owner_rows = jnp.broadcast_to(owner_row, (TILE, TILE))
    same = (owner_rows == owner_rows.T) & (iota(0) < iota(1))
    rank_row = jnp.sum(same.astype(F32), axis=0, keepdims=True)
    owner_int = owner[...]
    place_int = 8 * ((owner_int >> 1) & 7) + 2 * (owner_int >> 4) + (owner_int & 1)
    place_row = jnp.concatenate([place_int.astype(F32), padding], axis=1)
    slot_row = jnp.where(place_row >= 0.0, place_row + OWNERS * rank_row, -1.0)
    slots = (slot_row == iota(0).astype(F32)).astype(F32)
    selector = jnp.concatenate(
        [slots[:, :SELECT], pltpu.roll(slots, TILE - PAIRED, 1)[:, :SELECT]], axis=0
    ).astype(BF16)

    load(0).wait()

    def own(index, carry):
        for group in range(2):
            pair_up(0, group * GROUP + index)
        return carry

    lax.fori_loop(0, GROUP, own, 0)

    for copy in var_copies:
        copy.wait_recv()
    linear = var_mine[...] + var_got[0] + var_got[1] + var_got[2]
    held[pl.ds(PAIRED * FIELDS, (SELECT - PAIRED) * FIELDS), :] = jnp.zeros(
        ((SELECT - PAIRED) * FIELDS, TILE), F32
    )

    def by_half(rows, count):
        parts = [rows[i * MASKS:(i + 1) * MASKS] for i in range(count)]
        return [jnp.where(left((MASKS, TILE)), parts[i], parts[i + 1]) for i in range(0, count, 2)]

    def finish(part):
        def step(chunk, carry):
            for group in range(2):
                piece(1 - group, 1, part, chunk).wait_recv()
                piece(group, 2, part, chunk).wait_recv()

                def one(k, inner):
                    square = group * GROUP + chunk * SQUARES + k
                    landed = rows_of(part * GROUP + chunk * SQUARES + k)
                    united = (
                        buf[0, rows_of(part * PAIRED + square), :].astype(F32)
                        + got[1, 1 - group, landed, :].astype(F32)
                        + got[2, group, landed, :].astype(F32)
                    )
                    w_wide = jnp.concatenate([mask_weights(square), mask_weights(square + PAIRED)], axis=0).astype(F32)
                    w_square = w_wide * w_wide
                    w_high = w_square.astype(BF16).astype(F32)
                    w_parts = jnp.concatenate([w_high, w_square - w_high], axis=0).astype(BF16)
                    squared = united * united
                    high = squared.astype(BF16)
                    low = (squared - high.astype(F32)).astype(BF16)
                    (burden,) = by_half(
                        jnp.dot(w_wide.astype(BF16), united.astype(BF16), preferred_element_type=F32), 2
                    )
                    main = by_half(jnp.dot(w_parts, high, preferred_element_type=F32), 4)
                    rest = by_half(jnp.dot(w_parts, low, preferred_element_type=F32), 4)
                    trace = [
                        jnp.sum(jnp.where(lane == tile + 64, linear, 0.0), axis=1, keepdims=True)
                        for tile in (square, square + PAIRED)
                    ]
                    traces = jnp.where(left((MASKS, TILE)), trace[0], trace[1])
                    first = pl.multiple_of(square * FIELDS, FIELDS)
                    held[pl.ds(first, MASKS), :] = burden
                    held[pl.ds(first + MASKS, MASKS), :] = main[0] + (main[1] + rest[0]) - traces
                    return inner

                lax.fori_loop(0, SQUARES, one, 0, unroll=True)
            return carry

        lax.fori_loop(0, CHUNKS, step, 0)

    def payload(part):
        for row in range(FIELDS):
            tiles = held[pl.ds(row, SELECT, stride=FIELDS), :].astype(BF16)
            chosen = jnp.dot(selector, tiles, preferred_element_type=F32)
            near_tiles, far_tiles = chosen[:TILE], chosen[TILE:]
            wide[pl.ds(row, OWNERS, stride=FIELDS), :] = jnp.where(
                left((OWNERS, TILE)),
                near_tiles[:OWNERS] + swap(far_tiles[:OWNERS]),
                swap(near_tiles[OWNERS:]) + far_tiles[OWNERS:],
            )
        packed[part] = wide[...].astype(BF16).reshape(SIDE, SIDE, FIELDS, TILE)
        for k in range(1, SIDE):
            first_stage(part, k).start()
        relayed[part, 0] = packed[part, my_z]

    def first_stage(part, k):
        there = along_z(AWAY[k])
        return pltpu.make_async_remote_copy(
            src_ref=packed.at[part, there],
            dst_ref=relayed.at[part, k],
            send_sem=pay_send.at[part, k],
            recv_sem=pay_recv.at[part, k],
            device_id={"gene": owner_of(there, my_place)},
            device_id_type=MESH,
        )

    def second_stage(part, batch, k):
        there = across(k)
        rows = pl.ds(batch * BATCH, BATCH)
        return pltpu.make_async_remote_copy(
            src_ref=relayed.at[part, rows, there],
            dst_ref=arrived.at[part, k, rows],
            send_sem=relay_send.at[part, batch, k],
            recv_sem=relay_recv.at[part, batch, k],
            device_id={"gene": owner_of(my_z, there)},
            device_id_type=MESH,
        )

    def relay(part):
        for batch in range(SIDE // BATCH):
            for k in range(max(1, batch * BATCH), (batch + 1) * BATCH):
                first_stage(part, k).wait_recv()
            for k in range(1, SIDE):
                second_stage(part, batch, k).start()
            rows = slice(batch * BATCH, (batch + 1) * BATCH)
            arrived[part, 0, rows] = relayed[part, rows, my_place]

    finish(0)
    payload(0)
    send_up_to(17, 19)

    spreads = jnp.zeros((MASKS, TILE), F32)
    for half in range(2):
        cov_piece(1 - half, 1).wait_recv()
        cov_piece(half, 2).wait_recv()
        total = (
            cov_out[me, half].astype(F32)
            + cov_got[1, 1 - half].astype(F32)
            + cov_got[2, half].astype(F32)
        )
        for k in range(PAIRS // 2):
            square = total[k * TILE:(k + 1) * TILE, :]
            square = square * square
            row_at = PAIRS // 2 * TILE + k
            diagonal = total[row_at:row_at + 1, :]
            upper = jnp.where(iota(0) < iota(1), 2.0 * square, jnp.where(iota(0) == iota(1), square, 0.0))
            lower = jnp.where(iota(0) > iota(1), 2.0 * square, 0.0)
            first = me * OWN_TILES + half * (PAIRS // 2) + k
            for tile, part in ((first, upper), (first + PAIRS, lower)):
                w_wide = mask_weights(tile).astype(F32)
                w_square = w_wide * w_wide
                carried = jnp.dot(w_square, part, precision=HIGHEST, preferred_element_type=F32)
                if part is lower:
                    carried = carried + w_square * (diagonal * diagonal)
                spread = jnp.sum(carried * w_square, axis=1, keepdims=True)
                spreads = spreads + jnp.where(lane == tile, spread, 0.0)
    spread_mine[...] = spreads
    spread_copies = to_cohorts(spread_mine, spread_got, spread_send, spread_recv)
    for copy in spread_copies:
        copy.start()
    send_up_to(19, 20)
    relay(0)
    send_up_to(20, 21)
    for copy in spread_copies:
        copy.wait_recv()
    spreads = spreads + spread_got[0] + spread_got[1] + spread_got[2]

    facts = jnp.concatenate(
        [
            jnp.where(lane < 64, linear, 0.0),
            spreads,
            jnp.broadcast_to(gene_row, (MASKS, TILE)),
            jnp.zeros((64 - 3 * MASKS, TILE), F32),
        ],
        axis=0,
    )
    slot_facts = lax.dot_general(
        slots, facts, (((1,), (1,)), ((), ())), precision=HIGHEST, preferred_element_type=F32
    )
    stats[...] = jnp.concatenate([slot_facts[:OWNERS], slot_facts[OWNERS:]], axis=1).reshape(SIDE, SIDE, TILE)

    def first_stats(k):
        there = along_z(AWAY[k])
        return pltpu.make_async_remote_copy(
            src_ref=stats.at[there],
            dst_ref=stats_relayed.at[k],
            send_sem=stat_send.at[0, k],
            recv_sem=stat_recv.at[0, k],
            device_id={"gene": owner_of(there, my_place)},
            device_id_type=MESH,
        )

    def second_stats(k):
        there = across(k)
        return pltpu.make_async_remote_copy(
            src_ref=stats_turned.at[there],
            dst_ref=stats_got.at[k],
            send_sem=stat_send.at[1, k],
            recv_sem=stat_recv.at[1, k],
            device_id={"gene": owner_of(my_z, there)},
            device_id_type=MESH,
        )

    for k in range(1, SIDE):
        first_stats(k).start()
    stats_relayed[0] = stats[my_z]
    send_up_to(21, 22)
    for k in range(1, SIDE):
        first_stats(k).wait_recv()
    for place in range(SIDE):
        stats_turned[place] = stats_relayed[:, place, :]
    for k in range(1, SIDE):
        second_stats(k).start()
    stats_got[0] = stats_turned[my_place]

    send_up_to(22, len(order))
    finish(1)
    payload(1)

    for k in range(1, SIDE):
        second_stats(k).wait_recv()
    all_stats = stats_got[...].reshape(OWNERS, TILE)
    turned = jnp.concatenate([all_stats, jnp.zeros_like(all_stats)], axis=0).T
    gene_at = (iota(0, (GENES, OWNERS)) + 1).astype(F32)
    chosen_by = jnp.concatenate(
        [
            jnp.where(
                jnp.broadcast_to(turned[row:row + 1, :OWNERS], (GENES, OWNERS)) == gene_at, 1.0, 0.0
            )
            for row in (FIELDS, 64 + FIELDS)
        ],
        axis=0,
    )
    sums = jnp.dot(chosen_by, all_stats, precision=HIGHEST, preferred_element_type=F32)
    moments = sums[:GENES, :64] + sums[GENES:, 64:]
    doubled = jnp.where(iota(1, (GENES, 64)) >= MASKS, 2.0 * moments, moments)
    scale = 1.0 / jnp.sqrt(jnp.maximum(doubled, 1.0))
    chosen_by = chosen_by.astype(BF16)

    def gather(part):
        for batch in range(SIDE // BATCH):
            for k in range(1, SIDE):
                second_stage(part, batch, k).wait_recv()
        wide_got[...] = arrived[part].astype(F32).reshape(OWNERS * FIELDS, TILE)
        results = []
        for row in range(FIELDS):
            received = wide_got[pl.ds(row, OWNERS, stride=FIELDS), :].astype(BF16)
            both = jnp.dot(chosen_by, received, preferred_element_type=F32)
            if part == 0:
                total = both[:GENES] + swap(both[GENES:])
            else:
                total = swap(both[:GENES]) + both[GENES:]
            results.append(total * scale[:, row:row + 1])
        return results

    firsts = gather(0)
    for row in range(FIELDS):
        target = burden_out if row < MASKS else skat_out
        target[:, row % MASKS, :] = firsts[row]

    relay(1)
    seconds = gather(1)
    for row in range(FIELDS):
        target = burden_out if row < MASKS else skat_out
        target[:, row % MASKS, :] = jnp.where(left((GENES, TILE)), target[:, row % MASKS, :], seconds[row])

    for item in order[-FLIGHT:]:
        for way in range(2):
            copy_of(item, way).wait_send()
    for copy in var_copies + spread_copies:
        copy.wait_send()
    for k in range(1, SIDE):
        first_stats(k).wait_send()
        second_stats(k).wait_send()
        for part in range(2):
            first_stage(part, k).wait_send()
            for batch in range(SIDE // BATCH):
                second_stage(part, batch, k).wait_send()


def shards(scores, flips, presence, covs, membership, weights, tile_owner, tile_gene):
    vmem = pl.BlockSpec(memory_space=pltpu.VMEM)
    hbm = pl.BlockSpec(memory_space=pl.ANY)
    out = jax.ShapeDtypeStruct((GENES, MASKS, TILE), F32)
    dma = pltpu.SemaphoreType.DMA
    I32 = jnp.int32
    scratch = [
        pltpu.VMEM((TILES, TILE), I32),
        pltpu.VMEM((TILES, TILE), I32),
        pltpu.VMEM((MASKS, TILES * TILE), I32),
        pltpu.VMEM((TILES, TILE), F32),
        pltpu.VMEM((1, TILES), I32),
        pltpu.VMEM((1, TILES), I32),
        pltpu.VMEM((COHORTS, TILES * TILE, TILE), BF16),
        pltpu.VMEM((3, 2, 2 * GROUP * TILE, TILE), BF16),
        pltpu.VMEM((PAIRED * TILE, TILE), BF16),
        pltpu.VMEM((TILES, TILE, TILE), BF16),
        pltpu.VMEM((COHORTS, 2, COV_ROWS, TILE), BF16),
        pltpu.VMEM((3, 2, COV_ROWS, TILE), BF16),
        pltpu.VMEM((TILES, TILE), F32),
        pltpu.VMEM((TILES, TILE), F32),
        pltpu.VMEM((SELECT * FIELDS, TILE), F32),
        pltpu.VMEM((MASKS, TILE), F32),
        pltpu.VMEM((COHORTS - 1, MASKS, TILE), F32),
        pltpu.VMEM((MASKS, TILE), F32),
        pltpu.VMEM((COHORTS - 1, MASKS, TILE), F32),
        pltpu.VMEM((SIDE, SIDE, TILE), F32),
        pltpu.VMEM((SIDE, SIDE, TILE), F32),
        pltpu.VMEM((SIDE, SIDE, TILE), F32),
        pltpu.VMEM((SIDE, SIDE, TILE), F32),
        pltpu.VMEM((OWNERS * FIELDS, TILE), F32),
        pltpu.VMEM((2, SIDE, SIDE, FIELDS, TILE), BF16),
        pltpu.VMEM((2, SIDE, SIDE, FIELDS, TILE), BF16),
        pltpu.VMEM((2, SIDE, SIDE, FIELDS, TILE), BF16),
        pltpu.VMEM((OWNERS * FIELDS, TILE), F32),
        dma((6,)),
        dma((2, CHUNKS, 2)),
        dma((COHORTS,)),
        dma,
        dma((2, 3, 2, CHUNKS)),
        dma((2, 3, 2, CHUNKS)),
        dma((2, 3)),
        dma((2, 3)),
        dma((COHORTS - 1,)),
        dma((COHORTS - 1,)),
        dma((COHORTS - 1,)),
        dma((COHORTS - 1,)),
        dma((2, SIDE)),
        dma((2, SIDE)),
        dma((2, SIDE)),
        dma((2, SIDE)),
        dma((2, SIDE // BATCH, SIDE)),
        dma((2, SIDE // BATCH, SIDE)),
    ]
    return pl.pallas_call(
        kernel,
        out_shape=(out, out),
        in_specs=[hbm] * 8,
        out_specs=(vmem, vmem),
        scratch_shapes=scratch,
        compiler_params=pltpu.CompilerParams(
            collective_id=0, has_side_effects=True, vmem_limit_bytes=56 * 1024 * 1024
        ),
        cost_estimate=pl.CostEstimate(flops=500_000_000, bytes_accessed=9_000_000, transcendentals=0),
    )(
        scores,
        flips.reshape(TILES, TILE),
        presence.reshape(TILES, TILE),
        covs,
        membership,
        weights.reshape(TILES, TILE),
        tile_owner.reshape(1, TILES),
        tile_gene.reshape(1, TILES),
    )


def solution(mesh):
    return jax.shard_map(
        shards,
        mesh=mesh,
        in_specs=(
            P("cohort", "gene", None),
            P("cohort", "gene"),
            P("cohort", "gene"),
            P("cohort", "gene", None, None),
            P(None, "gene"),
            P("gene"),
            P("gene", None),
            P("gene"),
        ),
        out_specs=(P("gene", None, "cohort"), P("gene", None, "cohort")),
        check_vma=False,
    )
```

```python
import jax
import jax.numpy as jnp
from jax import lax
from jax.experimental import pallas as pl
from jax.experimental.pallas import tpu as pltpu
from jax.sharding import PartitionSpec as P

F32, BF16 = jnp.float32, jnp.bfloat16
MESH = pl.DeviceIdType.MESH
TILE = 128
TILES = 48
PAIRED = TILES // 2
HALF = TILE // 2
GROUP = PAIRED // 2
CHUNKS = 4
SQUARES = GROUP // CHUNKS
CHUNK_ROWS = SQUARES * TILE
COHORTS = 4
OWNERS = 64
SIDE = 8
BATCH = 4
AWAY = (0, 4, 3, 5, 2, 6, 1, 7)
GENES = 16
MASKS = 8
FIELDS = 2 * MASKS
OWN_TILES = TILES // COHORTS
PAIRS = OWN_TILES // 2
COV_ROWS = PAIRS // 2 * TILE + 16
FLIGHT = 3
SELECT = 32
HIGHEST = lax.Precision.HIGHEST


def rows_of(tile, count=1):
    return pl.ds(pl.multiple_of(tile * TILE, TILE), count * TILE)


def iota(axis, shape=(TILE, TILE)):
    return lax.broadcasted_iota(jnp.int32, shape, axis)


def swap(value):
    return pltpu.roll(value, HALF, 1)


def left(shape=(TILE, TILE)):
    return iota(1, shape) < HALF


def kernel(
    scores, flips_in, presence_in, covs, membership_in, weights_in, owner_in, gene_in,
    burden_out, skat_out,
    flips, presence, membership, weights, owner, gene,
    buf, got, factor_wide, cov_in, cov_out, cov_got, factor, sign, held,
    var_mine, var_got, spread_mine, spread_got, stats, stats_got,
    stats_relayed, stats_turned, wide, packed, relayed, arrived, wide_got,
    small_sem, far_sem, load_sem, cov_sem, send_sem, recv_sem, cov_send, cov_recv,
    var_send, var_recv, spread_send, spread_recv, stat_send, stat_recv, pay_send, pay_recv, relay_send, relay_recv,
):
    me = lax.axis_index("cohort")
    mine = lax.axis_index("gene")

    def cohort(relative):
        return lax.rem(me + relative, COHORTS)

    my_z = lax.rem(mine // 2, SIDE)
    my_place = 2 * (mine // 16) + lax.rem(mine, 2)

    def along_z(offset):
        return lax.rem(my_z + offset, SIDE)

    def across(offset):
        return lax.rem(my_place + offset, SIDE)

    def owner_of(z, place):
        return 16 * (place // 2) + 2 * z + lax.rem(place, 2)

    def columns(relative):
        return pl.ds(pl.multiple_of(cohort(relative) * TILE, TILE), TILE)

    def load(relative):
        return pltpu.make_async_copy(scores.at[0, :, columns(relative)], buf.at[relative], load_sem.at[relative])

    def load_far(group, chunk, second):
        rows = rows_of(second * PAIRED + group * GROUP + chunk * SQUARES, SQUARES)
        return pltpu.make_async_copy(
            scores.at[0, rows, columns(2)], buf.at[2, rows], far_sem.at[group, chunk, second]
        )

    pieces = ((flips_in, flips), (presence_in, presence), (membership_in, membership),
              (weights_in, weights), (owner_in, owner), (gene_in, gene))
    small = [pltpu.make_async_copy(source, target, small_sem.at[i]) for i, (source, target) in enumerate(pieces)]
    load_cov = pltpu.make_async_copy(covs.at[0], cov_in, cov_sem)
    barrier = pltpu.get_barrier_semaphore()
    for step in range(1, COHORTS):
        pl.semaphore_signal(barrier, inc=1, device_id={"cohort": cohort(step)}, device_id_type=MESH)

    for offset in range(1, SIDE):
        for there in (owner_of(along_z(offset), my_place), owner_of(my_z, across(offset))):
            pl.semaphore_signal(barrier, inc=1, device_id={"gene": there}, device_id_type=MESH)
    small[0].start()
    small[1].start()
    for chunk in range(CHUNKS):
        for group in range(2):
            for second in range(2):
                load_far(group, chunk, second).start()

    load(1).start()
    load(3).start()
    for copy in small[2:]:
        copy.start()
    load_cov.start()
    load(0).start()

    def piece(way, phase, part, chunk):
        group = 1 - way if phase == 1 else way
        relative = 2 if phase == 0 else (1 if way == 0 else 3)
        return pltpu.make_async_remote_copy(
            src_ref=buf.at[relative, rows_of(part * PAIRED + group * GROUP + chunk * SQUARES, SQUARES)],
            dst_ref=got.at[phase, way, rows_of(part * GROUP + chunk * SQUARES, SQUARES)],
            send_sem=send_sem.at[way, phase, part, chunk],
            recv_sem=recv_sem.at[way, phase, part, chunk],
            device_id={"cohort": cohort(1 if way == 0 else 3)},
            device_id_type=MESH,
        )

    def cov_piece(way, phase):
        half = 1 - way if phase == 1 else way
        relative = 2 if phase == 0 else (1 if way == 0 else 3)
        return pltpu.make_async_remote_copy(
            src_ref=cov_out.at[cohort(relative), half],
            dst_ref=cov_got.at[phase, way],
            send_sem=cov_send.at[way, phase],
            recv_sem=cov_recv.at[way, phase],
            device_id={"cohort": cohort(1 if way == 0 else 3)},
            device_id_type=MESH,
        )

    def pair_up(relative, square):
        first, second = rows_of(square), rows_of(square + PAIRED)
        x = buf[relative, first, :].astype(F32)
        y = buf[relative, second, :].astype(F32)
        sign_of = factor_wide[first, :].astype(F32)
        buf[relative, first, :] = (jnp.where(left(), x, swap(y)) * sign_of).astype(BF16)
        buf[relative, second, :] = (jnp.where(left(), swap(x), y) * sign_of).astype(BF16)

    def mask_weights(tile):
        member = membership[:, rows_of(tile)].astype(F32)
        return (weights[pl.ds(tile, 1), :] * (1.0 + 3.0 * member) / 4.0).astype(BF16)

    small[0].wait()
    small[1].wait()
    sign[...] = 1.0 - 2.0 * flips[...].astype(F32)
    factor[...] = sign[...] * presence[...].astype(F32)

    def far(group, chunk):
        load_far(group, chunk, 0).wait()
        load_far(group, chunk, 1).wait()

        def one(k, inner):
            square = group * GROUP + chunk * SQUARES + k
            x = jnp.broadcast_to(factor[pl.ds(square, 1), :], (TILE, TILE)).T
            y = jnp.broadcast_to(factor[pl.ds(square + PAIRED, 1), :], (TILE, TILE)).T
            factor_wide[rows_of(square), :] = jnp.where(left(), x, y).astype(BF16)
            pair_up(2, square)
            return inner

        lax.fori_loop(0, SQUARES, one, 0, unroll=True)

    far(0, 0)
    far(1, 0)
    pl.semaphore_wait(barrier, 2 * (SIDE - 1) + COHORTS - 1)
    piece(0, 0, 0, 0).start()
    piece(1, 0, 0, 0).start()

    def more_far(chunk, carry):
        for way in range(2):
            far(way, chunk)
            piece(way, 0, 0, chunk).start()
        return carry

    lax.fori_loop(1, CHUNKS, more_far, 0)

    for copy in small[2:]:
        copy.wait()
    load_cov.wait()
    lane = iota(1, (MASKS, TILE))

    def cov_group(group, linear):
        root, half = group // 2, lax.rem(group, 2)
        diagonals = jnp.zeros((16, TILE), F32)
        for k in range(PAIRS // 2):
            upper = root * OWN_TILES + half * (PAIRS // 2) + k
            signed = []
            for tile in (upper, upper + PAIRS):
                row = jnp.broadcast_to(sign[pl.ds(tile, 1), :], (TILE, TILE))
                block = cov_in[tile].astype(F32) * row * row.T
                diagonal = jnp.sum(jnp.where(iota(0) == iota(1), block, 0.0), axis=0, keepdims=True)
                w_rows = mask_weights(tile)
                w_wide = w_rows.astype(F32)
                carried = jnp.dot(w_rows, block.astype(BF16), preferred_element_type=F32)
                variance = jnp.sum(carried * w_wide, axis=1, keepdims=True)
                trace = jnp.sum(w_wide * w_wide * diagonal, axis=1, keepdims=True)
                linear = linear + jnp.where(lane == tile, variance, 0.0)
                linear = linear + jnp.where(lane == tile + 64, trace, 0.0)
                signed.append(block)
            diagonals = jnp.where(iota(0, (16, TILE)) == k, diagonal, diagonals)
            both = jnp.where(iota(0) <= iota(1), signed[0], signed[1])
            cov_out[root, half, k * TILE:(k + 1) * TILE, :] = both.astype(BF16)
        cov_out[root, half, PAIRS // 2 * TILE:, :] = diagonals.astype(BF16)
        return linear

    var_mine[...] = lax.fori_loop(0, 2 * COHORTS, cov_group, jnp.zeros((MASKS, TILE), F32))

    def to_cohorts(source, target, sent, received):
        return [
            pltpu.make_async_remote_copy(
                src_ref=source,
                dst_ref=target.at[step - 1],
                send_sem=sent.at[step - 1],
                recv_sem=received.at[step - 1],
                device_id={"cohort": cohort(step)},
                device_id_type=MESH,
            )
            for step in range(1, COHORTS)
        ]

    var_copies = to_cohorts(var_mine, var_got, var_send, var_recv)
    for copy in var_copies:
        copy.start()

    chunks = range(CHUNKS)
    order = [(0, 0, c) for c in chunks] + [(1, 0, c) for c in chunks] + [(0, None, 0), (1, None, 0)]
    order += [(2, 0, c) for c in chunks] + [(2, None, 0)]
    order += [(phase, 1, c) for phase in range(3) for c in chunks]

    def copy_of(item, way):
        phase, part, chunk = item
        return cov_piece(way, phase) if part is None else piece(way, phase, part, chunk)

    def prepare(item, way):
        phase, part, chunk = item
        relative = 1 if way == 0 else 3
        if part is None and phase == 2:
            cov_piece(way, 0).wait_recv()
            root = cohort(relative)
            cov_out[root, way] = (cov_out[root, way].astype(F32) + cov_got[0, way].astype(F32)).astype(BF16)
        elif part == 0 and phase == 1:
            for k in range(SQUARES):
                pair_up(relative, (1 - way) * GROUP + chunk * SQUARES + k)
        elif part is not None and phase == 2:
            piece(way, 0, part, chunk).wait_recv()
            for k in range(SQUARES):
                rows = rows_of(part * PAIRED + way * GROUP + chunk * SQUARES + k)
                landed = rows_of(part * GROUP + chunk * SQUARES + k)
                if part == 0:
                    pair_up(relative, way * GROUP + chunk * SQUARES + k)
                total = buf[relative, rows, :].astype(F32) + got[0, way, landed, :].astype(F32)
                buf[relative, rows, :] = total.astype(BF16)

    def send_up_to(first, end):
        for index in range(first, end):
            for way in range(2):
                prepare(order[index], way)
                copy_of(order[index - FLIGHT], way).wait_send()
                copy_of(order[index], way).start()

    load(1).wait()
    load(3).wait()
    for item in order[:CHUNKS - FLIGHT]:
        for way in range(2):
            copy_of(item, way).wait_send()
    send_up_to(CHUNKS, 17)

    padding = jnp.full((1, TILE - TILES), -1.0, F32)
    owner_row = jnp.concatenate([owner[...].astype(F32), padding], axis=1)
    gene_row = jnp.concatenate([gene[...].astype(F32), padding], axis=1) + 1.0
    owner_rows = jnp.broadcast_to(owner_row, (TILE, TILE))
    same = (owner_rows == owner_rows.T) & (iota(0) < iota(1))
    rank_row = jnp.sum(same.astype(F32), axis=0, keepdims=True)
    owner_int = owner[...]
    place_int = 8 * ((owner_int >> 1) & 7) + 2 * (owner_int >> 4) + (owner_int & 1)
    place_row = jnp.concatenate([place_int.astype(F32), padding], axis=1)
    slot_row = jnp.where(place_row >= 0.0, place_row + OWNERS * rank_row, -1.0)
    slots = (slot_row == iota(0).astype(F32)).astype(F32)
    selector = jnp.concatenate(
        [slots[:, :SELECT], pltpu.roll(slots, TILE - PAIRED, 1)[:, :SELECT]], axis=0
    ).astype(BF16)

    load(0).wait()

    def own(index, carry):
        for group in range(2):
            pair_up(0, group * GROUP + index)
        return carry

    lax.fori_loop(0, GROUP, own, 0)

    for copy in var_copies:
        copy.wait_recv()
    linear = var_mine[...] + var_got[0] + var_got[1] + var_got[2]
    held[pl.ds(PAIRED * FIELDS, (SELECT - PAIRED) * FIELDS), :] = jnp.zeros(
        ((SELECT - PAIRED) * FIELDS, TILE), F32
    )

    def by_half(rows, count):
        parts = [rows[i * MASKS:(i + 1) * MASKS] for i in range(count)]
        return [jnp.where(left((MASKS, TILE)), parts[i], parts[i + 1]) for i in range(0, count, 2)]

    def finish(part):
        def step(chunk, carry):
            for group in range(2):
                piece(1 - group, 1, part, chunk).wait_recv()
                piece(group, 2, part, chunk).wait_recv()

            def one(group, k):
                square = group * GROUP + chunk * SQUARES + k
                landed = rows_of(part * GROUP + chunk * SQUARES + k)
                united = (
                    buf[0, rows_of(part * PAIRED + square), :].astype(F32)
                    + got[1, 1 - group, landed, :].astype(F32)
                    + got[2, group, landed, :].astype(F32)
                )
                w_wide = jnp.concatenate([mask_weights(square), mask_weights(square + PAIRED)], axis=0).astype(F32)
                w_square = w_wide * w_wide
                w_high = w_square.astype(BF16).astype(F32)
                w_parts = jnp.concatenate([w_high, w_square - w_high], axis=0).astype(BF16)
                squared = united * united
                high = squared.astype(BF16)
                low = (squared - high.astype(F32)).astype(BF16)
                (burden,) = by_half(
                    jnp.dot(w_wide.astype(BF16), united.astype(BF16), preferred_element_type=F32), 2
                )
                main = by_half(jnp.dot(w_parts, high, preferred_element_type=F32), 4)
                rest = by_half(jnp.dot(w_parts, low, preferred_element_type=F32), 4)
                trace = [
                    jnp.sum(jnp.where(lane == tile + 64, linear, 0.0), axis=1, keepdims=True)
                    for tile in (square, square + PAIRED)
                ]
                traces = jnp.where(left((MASKS, TILE)), trace[0], trace[1])
                first = pl.multiple_of(square * FIELDS, FIELDS)
                held[pl.ds(first, MASKS), :] = burden
                held[pl.ds(first + MASKS, MASKS), :] = main[0] + (main[1] + rest[0]) - traces

            for k in range(SQUARES):
                for group in range(2):
                    one(group, k)
            return carry

        lax.fori_loop(0, CHUNKS, step, 0)

    def payload(part):
        for row in range(FIELDS):
            tiles = held[pl.ds(row, SELECT, stride=FIELDS), :].astype(BF16)
            chosen = jnp.dot(selector, tiles, preferred_element_type=F32)
            near_tiles, far_tiles = chosen[:TILE], chosen[TILE:]
            wide[pl.ds(row, OWNERS, stride=FIELDS), :] = jnp.where(
                left((OWNERS, TILE)),
                near_tiles[:OWNERS] + swap(far_tiles[:OWNERS]),
                swap(near_tiles[OWNERS:]) + far_tiles[OWNERS:],
            )
        packed[part] = wide[...].astype(BF16).reshape(SIDE, SIDE, FIELDS, TILE)
        for k in range(1, SIDE):
            first_stage(part, k).start()
        relayed[part, 0] = packed[part, my_z]

    def first_stage(part, k):
        there = along_z(AWAY[k])
        return pltpu.make_async_remote_copy(
            src_ref=packed.at[part, there],
            dst_ref=relayed.at[part, k],
            send_sem=pay_send.at[part, k],
            recv_sem=pay_recv.at[part, k],
            device_id={"gene": owner_of(there, my_place)},
            device_id_type=MESH,
        )

    def second_stage(part, batch, k):
        there = across(k)
        rows = pl.ds(batch * BATCH, BATCH)
        return pltpu.make_async_remote_copy(
            src_ref=relayed.at[part, rows, there],
            dst_ref=arrived.at[part, k, rows],
            send_sem=relay_send.at[part, batch, k],
            recv_sem=relay_recv.at[part, batch, k],
            device_id={"gene": owner_of(my_z, there)},
            device_id_type=MESH,
        )

    def relay(part):
        for batch in range(SIDE // BATCH):
            for k in range(max(1, batch * BATCH), (batch + 1) * BATCH):
                first_stage(part, k).wait_recv()
            for k in range(1, SIDE):
                second_stage(part, batch, k).start()
            rows = slice(batch * BATCH, (batch + 1) * BATCH)
            arrived[part, 0, rows] = relayed[part, rows, my_place]

    finish(0)
    payload(0)
    send_up_to(17, 19)

    spreads = jnp.zeros((MASKS, TILE), F32)
    for half in range(2):
        cov_piece(1 - half, 1).wait_recv()
        cov_piece(half, 2).wait_recv()
        total = (
            cov_out[me, half].astype(F32)
            + cov_got[1, 1 - half].astype(F32)
            + cov_got[2, half].astype(F32)
        )
        for k in range(PAIRS // 2):
            square = total[k * TILE:(k + 1) * TILE, :]
            square = square * square
            row_at = PAIRS // 2 * TILE + k
            diagonal = total[row_at:row_at + 1, :]
            upper = jnp.where(iota(0) < iota(1), 2.0 * square, jnp.where(iota(0) == iota(1), square, 0.0))
            lower = jnp.where(iota(0) > iota(1), 2.0 * square, 0.0)
            first = me * OWN_TILES + half * (PAIRS // 2) + k
            for tile, part in ((first, upper), (first + PAIRS, lower)):
                w_wide = mask_weights(tile).astype(F32)
                w_square = w_wide * w_wide
                carried = jnp.dot(w_square, part, precision=HIGHEST, preferred_element_type=F32)
                if part is lower:
                    carried = carried + w_square * (diagonal * diagonal)
                spread = jnp.sum(carried * w_square, axis=1, keepdims=True)
                spreads = spreads + jnp.where(lane == tile, spread, 0.0)
    spread_mine[...] = spreads
    spread_copies = to_cohorts(spread_mine, spread_got, spread_send, spread_recv)
    for copy in spread_copies:
        copy.start()
    send_up_to(19, 20)
    relay(0)
    send_up_to(20, 21)
    for copy in spread_copies:
        copy.wait_recv()
    spreads = spreads + spread_got[0] + spread_got[1] + spread_got[2]

    facts = jnp.concatenate(
        [
            jnp.where(lane < 64, linear, 0.0),
            spreads,
            jnp.broadcast_to(gene_row, (MASKS, TILE)),
            jnp.zeros((64 - 3 * MASKS, TILE), F32),
        ],
        axis=0,
    )
    slot_facts = lax.dot_general(
        slots, facts, (((1,), (1,)), ((), ())), precision=HIGHEST, preferred_element_type=F32
    )
    stats[...] = jnp.concatenate([slot_facts[:OWNERS], slot_facts[OWNERS:]], axis=1).reshape(SIDE, SIDE, TILE)

    def first_stats(k):
        there = along_z(AWAY[k])
        return pltpu.make_async_remote_copy(
            src_ref=stats.at[there],
            dst_ref=stats_relayed.at[k],
            send_sem=stat_send.at[0, k],
            recv_sem=stat_recv.at[0, k],
            device_id={"gene": owner_of(there, my_place)},
            device_id_type=MESH,
        )

    def second_stats(k):
        there = across(k)
        return pltpu.make_async_remote_copy(
            src_ref=stats_turned.at[there],
            dst_ref=stats_got.at[k],
            send_sem=stat_send.at[1, k],
            recv_sem=stat_recv.at[1, k],
            device_id={"gene": owner_of(my_z, there)},
            device_id_type=MESH,
        )

    for k in range(1, SIDE):
        first_stats(k).start()
    stats_relayed[0] = stats[my_z]
    send_up_to(21, 22)
    for k in range(1, SIDE):
        first_stats(k).wait_recv()
    for place in range(SIDE):
        stats_turned[place] = stats_relayed[:, place, :]
    for k in range(1, SIDE):
        second_stats(k).start()
    stats_got[0] = stats_turned[my_place]

    send_up_to(22, len(order))
    finish(1)
    payload(1)

    for k in range(1, SIDE):
        second_stats(k).wait_recv()
    all_stats = stats_got[...].reshape(OWNERS, TILE)
    turned = jnp.concatenate([all_stats, jnp.zeros_like(all_stats)], axis=0).T
    gene_at = (iota(0, (GENES, OWNERS)) + 1).astype(F32)
    chosen_by = jnp.concatenate(
        [
            jnp.where(
                jnp.broadcast_to(turned[row:row + 1, :OWNERS], (GENES, OWNERS)) == gene_at, 1.0, 0.0
            )
            for row in (FIELDS, 64 + FIELDS)
        ],
        axis=0,
    )
    sums = jnp.dot(chosen_by, all_stats, precision=HIGHEST, preferred_element_type=F32)
    moments = sums[:GENES, :64] + sums[GENES:, 64:]
    doubled = jnp.where(iota(1, (GENES, 64)) >= MASKS, 2.0 * moments, moments)
    scale = 1.0 / jnp.sqrt(jnp.maximum(doubled, 1.0))
    chosen_by = chosen_by.astype(BF16)

    def gather(part):
        for batch in range(SIDE // BATCH):
            for k in range(1, SIDE):
                second_stage(part, batch, k).wait_recv()
        wide_got[...] = arrived[part].astype(F32).reshape(OWNERS * FIELDS, TILE)
        results = []
        for row in range(FIELDS):
            received = wide_got[pl.ds(row, OWNERS, stride=FIELDS), :].astype(BF16)
            both = jnp.dot(chosen_by, received, preferred_element_type=F32)
            if part == 0:
                total = both[:GENES] + swap(both[GENES:])
            else:
                total = swap(both[:GENES]) + both[GENES:]
            results.append(total * scale[:, row:row + 1])
        return results

    firsts = gather(0)
    for row in range(FIELDS):
        target = burden_out if row < MASKS else skat_out
        target[:, row % MASKS, :] = firsts[row]

    relay(1)
    seconds = gather(1)
    for row in range(FIELDS):
        target = burden_out if row < MASKS else skat_out
        target[:, row % MASKS, :] = jnp.where(left((GENES, TILE)), target[:, row % MASKS, :], seconds[row])

    for item in order[-FLIGHT:]:
        for way in range(2):
            copy_of(item, way).wait_send()
    for copy in var_copies + spread_copies:
        copy.wait_send()
    for k in range(1, SIDE):
        first_stats(k).wait_send()
        second_stats(k).wait_send()
        for part in range(2):
            first_stage(part, k).wait_send()
            for batch in range(SIDE // BATCH):
                second_stage(part, batch, k).wait_send()


def shards(scores, flips, presence, covs, membership, weights, tile_owner, tile_gene):
    vmem = pl.BlockSpec(memory_space=pltpu.VMEM)
    hbm = pl.BlockSpec(memory_space=pl.ANY)
    out = jax.ShapeDtypeStruct((GENES, MASKS, TILE), F32)
    dma = pltpu.SemaphoreType.DMA
    I32 = jnp.int32
    scratch = [
        pltpu.VMEM((TILES, TILE), I32),
        pltpu.VMEM((TILES, TILE), I32),
        pltpu.VMEM((MASKS, TILES * TILE), I32),
        pltpu.VMEM((TILES, TILE), F32),
        pltpu.VMEM((1, TILES), I32),
        pltpu.VMEM((1, TILES), I32),
        pltpu.VMEM((COHORTS, TILES * TILE, TILE), BF16),
        pltpu.VMEM((3, 2, 2 * GROUP * TILE, TILE), BF16),
        pltpu.VMEM((PAIRED * TILE, TILE), BF16),
        pltpu.VMEM((TILES, TILE, TILE), BF16),
        pltpu.VMEM((COHORTS, 2, COV_ROWS, TILE), BF16),
        pltpu.VMEM((3, 2, COV_ROWS, TILE), BF16),
        pltpu.VMEM((TILES, TILE), F32),
        pltpu.VMEM((TILES, TILE), F32),
        pltpu.VMEM((SELECT * FIELDS, TILE), F32),
        pltpu.VMEM((MASKS, TILE), F32),
        pltpu.VMEM((COHORTS - 1, MASKS, TILE), F32),
        pltpu.VMEM((MASKS, TILE), F32),
        pltpu.VMEM((COHORTS - 1, MASKS, TILE), F32),
        pltpu.VMEM((SIDE, SIDE, TILE), F32),
        pltpu.VMEM((SIDE, SIDE, TILE), F32),
        pltpu.VMEM((SIDE, SIDE, TILE), F32),
        pltpu.VMEM((SIDE, SIDE, TILE), F32),
        pltpu.VMEM((OWNERS * FIELDS, TILE), F32),
        pltpu.VMEM((2, SIDE, SIDE, FIELDS, TILE), BF16),
        pltpu.VMEM((2, SIDE, SIDE, FIELDS, TILE), BF16),
        pltpu.VMEM((2, SIDE, SIDE, FIELDS, TILE), BF16),
        pltpu.VMEM((OWNERS * FIELDS, TILE), F32),
        dma((6,)),
        dma((2, CHUNKS, 2)),
        dma((COHORTS,)),
        dma,
        dma((2, 3, 2, CHUNKS)),
        dma((2, 3, 2, CHUNKS)),
        dma((2, 3)),
        dma((2, 3)),
        dma((COHORTS - 1,)),
        dma((COHORTS - 1,)),
        dma((COHORTS - 1,)),
        dma((COHORTS - 1,)),
        dma((2, SIDE)),
        dma((2, SIDE)),
        dma((2, SIDE)),
        dma((2, SIDE)),
        dma((2, SIDE // BATCH, SIDE)),
        dma((2, SIDE // BATCH, SIDE)),
    ]
    return pl.pallas_call(
        kernel,
        out_shape=(out, out),
        in_specs=[hbm] * 8,
        out_specs=(vmem, vmem),
        scratch_shapes=scratch,
        compiler_params=pltpu.CompilerParams(
            collective_id=0, has_side_effects=True, vmem_limit_bytes=56 * 1024 * 1024
        ),
        cost_estimate=pl.CostEstimate(flops=500_000_000, bytes_accessed=9_000_000, transcendentals=0),
    )(
        scores,
        flips.reshape(TILES, TILE),
        presence.reshape(TILES, TILE),
        covs,
        membership,
        weights.reshape(TILES, TILE),
        tile_owner.reshape(1, TILES),
        tile_gene.reshape(1, TILES),
    )


def solution(mesh):
    return jax.shard_map(
        shards,
        mesh=mesh,
        in_specs=(
            P("cohort", "gene", None),
            P("cohort", "gene"),
            P("cohort", "gene"),
            P("cohort", "gene", None, None),
            P(None, "gene"),
            P("gene"),
            P("gene", None),
            P("gene"),
        ),
        out_specs=(P("gene", None, "cohort"), P("gene", None, "cohort")),
        check_vma=False,
    )
```
